32 devices in a mesh: grp: 2 (over x), tm: 16 (over z, y, core).
Axes of the slice: x: 2, y: 2, z: 4, core: 2. Of those that a mesh axis runs over, the one named last changes fastest.
Arguments:
- frames_in: bfloat16 [16384, 1536], P(('grp', 'tm')), parts along dimension 0, may hold values from -6 to 6
- frame_time: int32 [64], P('grp'), parts along dimension 0, may hold values from 0 to 31, each once
- norm_gain: float32 [1536], replicated, may hold values from 0.25 to 1.75
- w_query: bfloat16 [1536, 768], replicated, may hold values from -2 to 2
- w_key: bfloat16 [1536, 768], replicated, may hold values from -2 to 2
- w_value: bfloat16 [1536, 768], replicated, may hold values from -0.15625 to 0.15625
- w_output: bfloat16 [768, 1536], replicated, may hold values from -0.21875 to 0.21875
Outputs:
- attended: bfloat16 [16384, 1536], P(('grp', 'tm')), parts along dimension 0
The draws below stay inside these ranges and needn't reach their ends.
There are 2 independent parts, one for each index of `grp`. The reference program is written for one: setup_inputs(seed, part) draws one part's arguments, and reference() takes and returns one part's arrays. A program takes and returns all parts, laid end to end along the dimension named above; an argument that names none is the same for every part. Nothing has to cross between parts.
Inputs may be any that keep to these rules, and one draw needn't show every extreme that they name: `frame_time`: each of 0 to 31 stands once.
All inputs are finite; a program needn't handle non-finite values.
Results may differ from the reference program's by a relative error of at most 0.004.
The reference program's roundings to bfloat16 on the way count: a program that leaves them out, or rounds other values in their place, can miss the bound.
Values may be sent and summed in bfloat16 or wider, within the bound.
No kernel may reach another device: no remote copies, remote signals or barrier semaphores. Data moves between devices by JAX's collectives and lax.ppermute only.
A program may use at most 128 MiB of HBM per device.

```python
import jax
import jax.numpy as jnp
from jax import lax

D = 1536
HEADS = 6
HD = 128
HH = 16
WW = 16
WIN = 8
POOL = 4
FRAMES = 32
PK = 16


def projection(key, salt):
    base = jnp.clip(jax.random.normal(jax.random.fold_in(key, salt), (D, HEADS * HD), jnp.float32), -6.0, 6.0) * D ** (-0.5)
    return jnp.clip(base, -2.0, 2.0)


def draw_w_query(key, part):
    return projection(key, 1).astype(jnp.bfloat16)


def draw_w_key(key, part):
    return projection(key, 2).astype(jnp.bfloat16)


def shard_levels(key, extent, split, smallest, top_value):
    def one(position, parts):
        steps = jax.random.uniform(jax.random.fold_in(jax.random.fold_in(key, 6), position), (parts,), jnp.float32, smallest / len(split), top_value / len(split))
        return jnp.repeat(jnp.exp(steps), extent[position] // parts).reshape((-1,) + (1,) * (len(extent) - position - 1))

    factor_of = one(*split[0])
    for cut in split[1:]:
        factor_of = factor_of * one(*cut)
    return factor_of


def normal_values(key, shape, deviation, reach, cuts=(), kind=jnp.bfloat16):
    result = jax.random.normal(key, shape, jnp.float32) * deviation
    if len(cuts) > 0:
        result = shard_levels(key, shape, cuts, -0.22, 0.18) * result
    return jnp.clip(result, min=-reach, max=reach).astype(kind)


def setup_inputs(seed: int = 0, part: int = 0) -> dict:
    key_of = jax.random.split(jax.random.key(seed), 8)
    part_keys = jax.random.split(jax.random.fold_in(key_of[7], part), 8)
    frames_in = normal_values(part_keys[0], (FRAMES * HH * WW, D), 1.0, 6.0, ((0, 16),))
    frame_time = jax.random.permutation(part_keys[1], FRAMES).astype(jnp.int32)
    norm_gain = jnp.clip(1.0 + 0.15 * jax.random.normal(key_of[2], (D,), jnp.float32), 0.25, 1.75)
    w_query = draw_w_query(jax.random.fold_in(key_of[7], 71), part)
    w_key = draw_w_key(jax.random.fold_in(key_of[7], 71), part)
    w_value = normal_values(key_of[5], (D, HEADS * HD), D ** -0.5, 0.15625)
    w_output = normal_values(key_of[6], (HEADS * HD, D), (HEADS * HD) ** -0.5, 0.21875)
    return {"frames_in": frames_in, "frame_time": frame_time, "norm_gain": norm_gain, "w_query": w_query, "w_key": w_key, "w_value": w_value, "w_output": w_output}


def normed_rows(frames_in, norm_gain):
    values_f = frames_in.astype(jnp.float32)
    scale = lax.rsqrt(lax.optimization_barrier(jnp.mean(values_f * values_f, axis=-1, keepdims=True)) + 1e-06)
    return (values_f * scale * norm_gain.astype(jnp.float32)).astype(jnp.bfloat16)

def to_windows(array, count):
    shaped = array.reshape(count, HH // WIN, WIN, WW // WIN, WIN, HEADS, HD)
    shaped = shaped.transpose(0, 1, 3, 2, 4, 5, 6)
    return shaped.reshape(count, HH // WIN * (WW // WIN), WIN * WIN, HEADS, HD)

def from_windows(array, count):
    shaped = array.reshape(count, HH // WIN, WW // WIN, WIN, WIN, HEADS * HD)
    shaped = shaped.transpose(0, 1, 3, 2, 4, 5)
    return shaped.reshape(count * HH * WW, HEADS * HD)

def pooled(array, count):
    shaped = array.reshape(count, HH // POOL, POOL, WW // POOL, POOL, HEADS * HD).astype(jnp.float32)
    return lax.optimization_barrier(jnp.mean(shaped, axis=(2, 4))).reshape(count * PK, HEADS, HD).astype(jnp.bfloat16)

def reference(frames_in, frame_time, norm_gain, w_query, w_key, w_value, w_output):
    count = frame_time.shape[0]
    normed = normed_rows(frames_in, norm_gain)
    query = jnp.dot(normed, w_query, preferred_element_type=jnp.float32).astype(jnp.bfloat16)
    keys = jnp.dot(normed, w_key, preferred_element_type=jnp.float32).astype(jnp.bfloat16)
    values = jnp.dot(normed, w_value, preferred_element_type=jnp.float32).astype(jnp.bfloat16)
    pooled_keys = lax.optimization_barrier(pooled(keys, count)).astype(jnp.float32)
    pooled_values = lax.optimization_barrier(pooled(values, count)).astype(jnp.float32)
    key_time = jnp.repeat(frame_time, PK)
    query_win = to_windows(query, count)
    keys_win = to_windows(keys, count)
    values_win = to_windows(values, count)
    factor = 1.0 / HD ** 0.5

    def one_frame(items):
        q_frame, k_frame, v_frame, t_frame = items
        q32 = q_frame.astype(jnp.float32)
        local_s = jnp.einsum('nqhd,nkhd->nhqk', q32, k_frame.astype(jnp.float32)) * factor
        far_s = jnp.einsum('nqhd,khd->nhqk', q32, pooled_keys) * factor
        valid = key_time < t_frame
        far_s = jnp.where(valid, far_s, -1e+30)
        top = jnp.maximum(lax.optimization_barrier(jnp.max(local_s, -1)), lax.optimization_barrier(jnp.max(far_s, -1)))
        local_w = jnp.exp(local_s - top[..., None])
        far_w = jnp.where(valid, jnp.exp(far_s - top[..., None]), 0.0)
        total = lax.optimization_barrier(jnp.sum(local_w, -1)) + lax.optimization_barrier(jnp.sum(far_w, -1))
        local_p = lax.optimization_barrier(local_w.astype(jnp.bfloat16)).astype(jnp.float32)
        far_p = lax.optimization_barrier(far_w.astype(jnp.bfloat16)).astype(jnp.float32)
        acc = jnp.einsum('nhqk,nkhd->nhqd', local_p, v_frame.astype(jnp.float32))
        acc = acc + jnp.einsum('nhqk,khd->nhqd', far_p, pooled_values)
        mixed = acc / total[..., None]
        return mixed.transpose(0, 2, 1, 3).astype(jnp.bfloat16)
    mixed = lax.map(one_frame, (query_win, keys_win, values_win, frame_time))
    mixed = from_windows(mixed, count)
    return jnp.dot(mixed, w_output, preferred_element_type=jnp.float32).astype(jnp.bfloat16)
```

```python
import functools
import math

import jax
import jax.numpy as jnp
from jax import lax
from jax.experimental import pallas as pl
from jax.experimental.pallas import tpu as pltpu
from jax.sharding import PartitionSpec as P

HEADS = 6
HD = 128
HH = 16
WW = 16
WIN = 8
POOL = 4
TOKENS = HH * WW
SLOTS = TOKENS // (POOL * POOL)
FAR = -1e30
SCALE = HD**-0.5 * math.log2(math.e)
F32 = jnp.float32
BF16 = jnp.bfloat16
VMEM = pl.BlockSpec(memory_space=pltpu.VMEM)
SMEM = pl.BlockSpec(memory_space=pltpu.SMEM)
HBM = pl.BlockSpec(memory_space=pl.ANY)


def exchange_plan(n):
    high = [1 << b for b in range(n.bit_length() - 2, 0, -1)]
    first = [high[0]] + high[2:] + high[1:2]
    second = high[1:2] + high[:1] + high[2:]
    held = [[0], [0]]
    for a, b in zip(first, second):
        held = [held[0] + [m ^ a for m in held[0]], held[1] + [m ^ b for m in held[1]]]
    return list(zip(first, second)), held


def norm_kernel(frames_hbm, gain_ref, wk_hbm, wv_hbm, normed_ref, pooled_ref, x_buf, wk_buf, wv_buf, x_sem, w_sem):
    rows, width = x_buf.shape
    parts = x_sem.shape[0]
    step = rows // parts
    loads = [
        pltpu.make_async_copy(frames_hbm.at[pl.ds(i * step, step)], x_buf.at[pl.ds(i * step, step)], x_sem.at[i])
        for i in range(parts)
    ]
    weights = [
        pltpu.make_async_copy(wk_hbm, wk_buf, w_sem.at[0]),
        pltpu.make_async_copy(wv_hbm, wv_buf, w_sem.at[1]),
    ]
    for copy in loads + weights:
        copy.start()
    gain = gain_ref[...]
    pair = 2 * WW
    per_window = WIN * WIN
    for i in range(parts):
        loads[i].wait()
        for g in range(i * step // pair, (i + 1) * step // pair):
            x = x_buf[pl.ds(g * pair, pair), :].astype(F32)
            scale = lax.rsqrt(jnp.mean(x * x, axis=-1, keepdims=True) + 1e-06)
            y = x * scale * gain
            frame, row = divmod(2 * g, HH)
            wr, r = divmod(row, WIN)
            for wc in range(WW // WIN):
                both = jnp.concatenate(
                    [y[wc * WIN : (wc + 1) * WIN], y[WW + wc * WIN : WW + (wc + 1) * WIN]], axis=0
                )
                base = frame * TOKENS + (wr * (WW // WIN) + wc) * per_window + r * WIN
                normed_ref[pl.ds(base, 2 * WIN), :] = both.astype(BF16)
    count = rows // TOKENS
    out_rows = count * SLOTS
    slot = lax.broadcasted_iota(jnp.int32, (out_rows, rows), 0)
    token = lax.broadcasted_iota(jnp.int32, (out_rows, rows), 1)
    r, c = token % per_window // WIN, token % WIN
    home = token // per_window * 4 + r // POOL * 2 + c // POOL
    pick = jnp.where(home == slot, 1.0 / (POOL * POOL), 0.0).astype(BF16)
    mean = jnp.dot(pick, normed_ref[...], preferred_element_type=F32)
    high = mean.astype(BF16)
    low = (mean - high.astype(F32)).astype(BF16)
    both = jnp.concatenate([high, low], axis=0)
    for i, buf in enumerate((wk_buf, wv_buf)):
        weights[i].wait()
        z = jnp.dot(both, buf[...], preferred_element_type=F32)
        cols = HEADS * HD
        pooled_ref[:, i * cols : (i + 1) * cols] = (z[:out_rows] + z[out_rows:]).astype(BF16)


def norm_and_pool(frames, gain, w_key, w_value):
    rows, width = frames.shape
    out_rows = rows // TOKENS * SLOTS
    cols = HEADS * HD
    return pl.pallas_call(
        norm_kernel,
        out_shape=(
            jax.ShapeDtypeStruct((rows, width), BF16),
            jax.ShapeDtypeStruct((out_rows, 2 * cols), BF16),
        ),
        in_specs=[HBM, VMEM, HBM, HBM],
        out_specs=(VMEM, VMEM),
        scratch_shapes=[
            pltpu.VMEM((rows, width), BF16),
            pltpu.VMEM((width, cols), BF16),
            pltpu.VMEM((width, cols), BF16),
            pltpu.SemaphoreType.DMA((4,)),
            pltpu.SemaphoreType.DMA((2,)),
        ],
        compiler_params=pltpu.CompilerParams(vmem_limit_bytes=24 << 20),
        cost_estimate=pl.CostEstimate(flops=400_000_000, bytes_accessed=8_000_000, transcendentals=0),
        name="norm_and_pool",
    )(frames, gain.reshape(1, width), w_key, w_value)


def own_block(me, mask_pair):
    a, b = mask_pair
    return me ^ (a if a == b else jnp.where(me % 2 == 0, a, b))


def mask_columns(time_ref, masks, count):
    me = lax.axis_index("tm")
    lane = lax.broadcasted_iota(jnp.int32, (SLOTS, HD), 1)
    own = [time_ref[me * count + f] for f in range(count)]
    tiles = []
    for pair in masks:
        source = own_block(me, pair)
        for g in range(count):
            t = time_ref[source * count + g]
            tile = jnp.zeros((SLOTS, HD), F32)
            for f in range(count):
                tile = jnp.where(lane == f, jnp.where(t < own[f], 0.0, FAR), tile)
            tiles.append(tile)
    return jnp.concatenate(tiles, axis=0).astype(BF16)


def frame_columns(tokens):
    frame = lax.broadcasted_iota(jnp.int32, (tokens, HD), 0) // TOKENS
    lane = lax.broadcasted_iota(jnp.int32, (tokens, HD), 1)
    return jnp.where(frame == lane, 1.0, 0.0).astype(BF16)


def dot_nt(a, b):
    return lax.dot_general(a, b, (((1,), (1,)), ((), ())), preferred_element_type=F32)


def dot_tn(a, b):
    return lax.dot_general(a, b, (((0,), (0,)), ((), ())), preferred_element_type=F32)


def head(h, base=0):
    return slice(base + h * HD, base + (h + 1) * HD)


def first_kernel(masks, time_ref, q_ref, k_ref, v_ref, near_ref, other_ref, acc_ref, m_ref, l_ref):
    tokens = q_ref.shape[0]
    count = tokens // TOKENS
    per_window = WIN * WIN
    cols = HEADS * HD
    bias = mask_columns(time_ref, masks, count)
    frames = frame_columns(tokens)
    left = lax.broadcasted_iota(jnp.int32, (per_window, 2 * per_window), 1) < per_window
    for h in range(HEADS):
        q = q_ref[:, head(h)]
        far_k = jnp.concatenate([near_ref[:, head(h)], other_ref[:, head(h)]], axis=0)
        far_v = jnp.concatenate([near_ref[:, head(h, cols)], other_ref[:, head(h, cols)]], axis=0)
        far_s = dot_nt(jnp.concatenate([far_k, bias], axis=1), jnp.concatenate([q, frames], axis=1))
        parts = []
        for w in range(tokens // (2 * per_window)):
            two = pl.ds(w * 2 * per_window, 2 * per_window)
            s = dot_nt(k_ref[two, head(h)], q_ref[two, head(h)])
            parts.append(jnp.where(left, s[:per_window], s[per_window:]))
        local_s = jnp.concatenate(parts, axis=1)
        top = jnp.maximum(jnp.max(local_s, axis=0, keepdims=True), jnp.max(far_s, axis=0, keepdims=True))
        local_w = jnp.exp2((local_s - top) * SCALE)
        far_w = jnp.exp2((far_s - top) * SCALE)
        total = jnp.sum(local_w, axis=0, keepdims=True) + jnp.sum(far_w, axis=0, keepdims=True)
        acc = dot_tn(far_v, far_w.astype(BF16))
        parts = []
        for w in range(tokens // (2 * per_window)):
            two = pl.ds(w * 2 * per_window, 2 * per_window)
            p = local_w[:, w * 2 * per_window : (w + 1) * 2 * per_window]
            p = jnp.concatenate([jnp.where(left, p, 0.0), jnp.where(left, 0.0, p)], axis=0).astype(BF16)
            parts.append(dot_tn(v_ref[two, head(h)], p))
        acc_ref[head(h), :] = acc + jnp.concatenate(parts, axis=1)
        m_ref[h : h + 1, :] = top
        l_ref[h : h + 1, :] = total


def far_step(h, q_ref, far_ref, bias, frames, m, l, acc):
    cols = HEADS * HD
    s = dot_nt(
        jnp.concatenate([far_ref[:, head(h)], bias], axis=1),
        jnp.concatenate([q_ref[:, head(h)], frames], axis=1),
    )
    top = jnp.maximum(m, jnp.max(s, axis=0, keepdims=True))
    w = jnp.exp2((s - top) * SCALE)
    keep = jnp.exp2((m - top) * SCALE)
    l = l * keep + jnp.sum(w, axis=0, keepdims=True)
    acc = acc * keep + dot_tn(far_ref[:, head(h, cols)], w.astype(BF16))
    return top, l, acc


def middle_kernel(masks, time_ref, q_ref, far_ref, acc_in, m_in, l_in, acc_ref, m_ref, l_ref):
    tokens = q_ref.shape[0]
    bias = mask_columns(time_ref, masks, tokens // TOKENS)
    frames = frame_columns(tokens)
    for h in range(HEADS):
        m, l, acc = far_step(
            h, q_ref, far_ref, bias, frames, m_in[h : h + 1, :], l_in[h : h + 1, :], acc_in[head(h), :]
        )
        acc_ref[head(h), :] = acc
        m_ref[h : h + 1, :] = m
        l_ref[h : h + 1, :] = l


def last_kernel(masks, time_ref, q_ref, far_ref, acc_in, m_in, l_in, wo_ref, out_ref, mixed, rows_buf):
    tokens = q_ref.shape[0]
    bias = mask_columns(time_ref, masks, tokens // TOKENS)
    frames = frame_columns(tokens)
    for h in range(HEADS):
        m, l, acc = far_step(
            h, q_ref, far_ref, bias, frames, m_in[h : h + 1, :], l_in[h : h + 1, :], acc_in[head(h), :]
        )
        mixed[:, head(h)] = jnp.transpose(acc * (1.0 / l))
    per_window = WIN * WIN
    for row in range(tokens // WW):
        frame, rest = divmod(row, HH)
        wr, r = divmod(rest, WIN)
        base = frame * TOKENS + wr * (WW // WIN) * per_window + r * WIN
        line = jnp.concatenate([mixed[pl.ds(base + wc * per_window, WIN), :] for wc in range(WW // WIN)], axis=0)
        rows_buf[pl.ds(row * WW, WW), :] = line.astype(BF16)
    out_ref[...] = jnp.dot(rows_buf[...], wo_ref[...], preferred_element_type=F32).astype(BF16)


def on_device(n, frames_in, frame_time, norm_gain, w_query, w_key, w_value, w_output):
    rows = frames_in.shape[0]
    cols = HEADS * HD
    phases, held = exchange_plan(n)
    normed, block = norm_and_pool(frames_in, norm_gain, w_key, w_value)

    def send(x, pair):
        return lax.ppermute(x, "tm", [(i, i ^ pair[i % 2]) for i in range(n)])

    for pair in phases[:-1]:
        block = jnp.concatenate([block, send(block, pair)], axis=0)
    late = send(block, phases[-1])
    other = send(block, (1, 1))
    other_late = send(late, (1, 1))
    half = len(held[0]) // 2
    own = list(zip(held[0], held[1]))
    far = [(a ^ 1, b ^ 1) for b, a in own]

    query, keys, values = (
        jnp.dot(normed, w, preferred_element_type=F32).astype(BF16) for w in (w_query, w_key, w_value)
    )
    state = (
        jax.ShapeDtypeStruct((cols, rows), F32),
        jax.ShapeDtypeStruct((8, rows), F32),
        jax.ShapeDtypeStruct((8, rows), F32),
    )
    params = pltpu.CompilerParams(vmem_limit_bytes=32 << 20)
    acc, m, l = pl.pallas_call(
        functools.partial(first_kernel, own[:half] + far[:half]),
        out_shape=state,
        in_specs=[SMEM] + [VMEM] * 5,
        out_specs=(VMEM, VMEM, VMEM),
        compiler_params=params,
        cost_estimate=pl.CostEstimate(flops=900_000_000, bytes_accessed=5_000_000, transcendentals=1_000_000),
        name="local_and_first",
    )(frame_time, query, keys, values, block, other)
    acc, m, l = pl.pallas_call(
        functools.partial(middle_kernel, own[half:]),
        out_shape=state,
        in_specs=[SMEM] + [VMEM] * 5,
        out_specs=(VMEM, VMEM, VMEM),
        input_output_aliases={3: 0, 4: 1, 5: 2},
        compiler_params=params,
        cost_estimate=pl.CostEstimate(flops=500_000_000, bytes_accessed=5_000_000, transcendentals=400_000),
        name="middle",
    )(frame_time, query, late, acc, m, l)
    return pl.pallas_call(
        functools.partial(last_kernel, far[half:]),
        out_shape=jax.ShapeDtypeStruct((rows, w_output.shape[1]), BF16),
        in_specs=[SMEM] + [VMEM] * 6,
        out_specs=VMEM,
        scratch_shapes=[pltpu.VMEM((rows, cols), F32), pltpu.VMEM((rows, cols), BF16)],
        compiler_params=params,
        cost_estimate=pl.CostEstimate(flops=1_700_000_000, bytes_accessed=8_000_000, transcendentals=400_000),
        name="last_and_output",
    )(frame_time, query, other_late, acc, m, l, w_output)


def solution(mesh):
    placed = (P(("grp", "tm"), None), P("grp"), P(), P(), P(), P(), P())
    return jax.shard_map(
        functools.partial(on_device, mesh.shape["tm"]),
        mesh=mesh,
        in_specs=placed,
        out_specs=P(("grp", "tm"), None),
        check_vma=False,
    )
```

```python
import functools
import math

import jax
import jax.numpy as jnp
from jax import lax
from jax.experimental import pallas as pl
from jax.experimental.pallas import tpu as pltpu
from jax.sharding import PartitionSpec as P

HEADS = 6
HD = 128
HH = 16
WW = 16
WIN = 8
POOL = 4
TOKENS = HH * WW
SLOTS = TOKENS // (POOL * POOL)
FAR = -1e30
SCALE = HD**-0.5 * math.log2(math.e)
F32 = jnp.float32
BF16 = jnp.bfloat16
VMEM = pl.BlockSpec(memory_space=pltpu.VMEM)
SMEM = pl.BlockSpec(memory_space=pltpu.SMEM)
HBM = pl.BlockSpec(memory_space=pl.ANY)


def exchange_plan(n):
    high = [1 << b for b in range(n.bit_length() - 2, 0, -1)]
    first = [high[0]] + high[2:] + high[1:2]
    second = high[1:2] + high[:1] + high[2:]
    held = [[0], [0]]
    for a, b in zip(first, second):
        held = [held[0] + [m ^ a for m in held[0]], held[1] + [m ^ b for m in held[1]]]
    return list(zip(first, second)), held


def norm_kernel(
    frames_hbm, gain_hbm, wk_hbm, wv_hbm, normed_ref, pooled_ref, x_buf, gain_buf, wk_buf, wv_buf, x_sem, g_sem, w_sem
):
    rows, width = x_buf.shape
    parts = x_sem.shape[0]
    step = rows // parts
    slabs = w_sem.shape[1]
    deep = width // slabs
    gain_load = pltpu.make_async_copy(gain_hbm, gain_buf.at[0], g_sem)
    loads = [
        pltpu.make_async_copy(frames_hbm.at[pl.ds(i * step, step)], x_buf.at[pl.ds(i * step, step)], x_sem.at[i])
        for i in range(parts)
    ]
    weights = [
        [
            pltpu.make_async_copy(w.at[pl.ds(j * deep, deep)], buf.at[pl.ds(j * deep, deep)], w_sem.at[i, j])
            for j in range(slabs)
        ]
        for i, (w, buf) in enumerate(((wk_hbm, wk_buf), (wv_hbm, wv_buf)))
    ]
    gain_load.start()
    for copy in loads:
        copy.start()
    for j in range(slabs):
        for i in range(2):
            weights[i][j].start()
    gain_load.wait()
    gain = gain_buf[...]
    pair = 2 * WW
    per_window = WIN * WIN
    for i in range(parts):
        loads[i].wait()
        for g in range(i * step // pair, (i + 1) * step // pair):
            x = x_buf[pl.ds(g * pair, pair), :].astype(F32)
            scale = lax.rsqrt(jnp.mean(x * x, axis=-1, keepdims=True) + 1e-06)
            y = x * scale * gain
            frame, row = divmod(2 * g, HH)
            wr, r = divmod(row, WIN)
            for wc in range(WW // WIN):
                both = jnp.concatenate(
                    [y[wc * WIN : (wc + 1) * WIN], y[WW + wc * WIN : WW + (wc + 1) * WIN]], axis=0
                )
                base = frame * TOKENS + (wr * (WW // WIN) + wc) * per_window + r * WIN
                normed_ref[pl.ds(base, 2 * WIN), :] = both.astype(BF16)
    count = rows // TOKENS
    out_rows = count * SLOTS
    slot = lax.broadcasted_iota(jnp.int32, (out_rows, rows), 0)
    token = lax.broadcasted_iota(jnp.int32, (out_rows, rows), 1)
    r, c = token % per_window // WIN, token % WIN
    home = token // per_window * 4 + r // POOL * 2 + c // POOL
    pick = jnp.where(home == slot, 1.0 / (POOL * POOL), 0.0).astype(BF16)
    mean = jnp.dot(pick, normed_ref[...], preferred_element_type=F32)
    high = mean.astype(BF16)
    low = (mean - high.astype(F32)).astype(BF16)
    both = jnp.concatenate([high, low], axis=0)
    cols = HEADS * HD
    total = [0.0, 0.0]
    for j in range(slabs):
        for i, buf in enumerate((wk_buf, wv_buf)):
            weights[i][j].wait()
            part = slice(j * deep, (j + 1) * deep)
            total[i] += jnp.dot(both[:, part], buf[part, :], preferred_element_type=F32)
    for i in range(2):
        pooled_ref[:, i * cols : (i + 1) * cols] = (total[i][:out_rows] + total[i][out_rows:]).astype(BF16)


def norm_and_pool(frames, gain, w_key, w_value):
    rows, width = frames.shape
    out_rows = rows // TOKENS * SLOTS
    cols = HEADS * HD
    return pl.pallas_call(
        norm_kernel,
        out_shape=(
            jax.ShapeDtypeStruct((rows, width), BF16),
            jax.ShapeDtypeStruct((out_rows, 2 * cols), BF16),
        ),
        in_specs=[HBM] * 4,
        out_specs=(VMEM, VMEM),
        scratch_shapes=[
            pltpu.VMEM((rows, width), BF16),
            pltpu.VMEM((1, width), F32),
            pltpu.VMEM((width, cols), BF16),
            pltpu.VMEM((width, cols), BF16),
            pltpu.SemaphoreType.DMA((4,)),
            pltpu.SemaphoreType.DMA,
            pltpu.SemaphoreType.DMA((2, 4)),
        ],
        compiler_params=pltpu.CompilerParams(vmem_limit_bytes=24 << 20),
        cost_estimate=pl.CostEstimate(flops=400_000_000, bytes_accessed=8_000_000, transcendentals=0),
        name="norm_and_pool",
    )(*(pltpu.with_memory_space_constraint(x, pltpu.HBM) for x in (frames, gain, w_key, w_value)))


def own_block(me, mask_pair):
    a, b = mask_pair
    return me ^ (a if a == b else jnp.where(me % 2 == 0, a, b))


def mask_columns(time_ref, masks, count):
    me = lax.axis_index("tm")
    lane = lax.broadcasted_iota(jnp.int32, (SLOTS, HD), 1)
    own = [time_ref[me * count + f] for f in range(count)]
    tiles = []
    for pair in masks:
        source = own_block(me, pair)
        for g in range(count):
            t = time_ref[source * count + g]
            tile = jnp.zeros((SLOTS, HD), F32)
            for f in range(count):
                tile = jnp.where(lane == f, jnp.where(t < own[f], 0.0, FAR), tile)
            tiles.append(tile)
    return jnp.concatenate(tiles, axis=0).astype(BF16)


def frame_columns(tokens):
    frame = lax.broadcasted_iota(jnp.int32, (tokens, HD), 0) // TOKENS
    lane = lax.broadcasted_iota(jnp.int32, (tokens, HD), 1)
    return jnp.where(frame == lane, 1.0, 0.0).astype(BF16)


def dot_nt(a, b):
    return lax.dot_general(a, b, (((1,), (1,)), ((), ())), preferred_element_type=F32)


def dot_tn(a, b):
    return lax.dot_general(a, b, (((0,), (0,)), ((), ())), preferred_element_type=F32)


def head(h, base=0):
    return slice(base + h * HD, base + (h + 1) * HD)


def first_kernel(masks, time_ref, q_ref, k_ref, v_ref, near_ref, other_ref, acc_ref, m_ref, l_ref):
    tokens = q_ref.shape[0]
    count = tokens // TOKENS
    per_window = WIN * WIN
    cols = HEADS * HD
    bias = mask_columns(time_ref, masks, count)
    frames = frame_columns(tokens)
    left = lax.broadcasted_iota(jnp.int32, (per_window, 2 * per_window), 1) < per_window
    for h in range(HEADS):
        q = q_ref[:, head(h)]
        far_k = jnp.concatenate([near_ref[:, head(h)], other_ref[:, head(h)]], axis=0)
        far_v = jnp.concatenate([near_ref[:, head(h, cols)], other_ref[:, head(h, cols)]], axis=0)
        far_s = dot_nt(jnp.concatenate([far_k, bias], axis=1), jnp.concatenate([q, frames], axis=1))
        parts = []
        for w in range(tokens // (2 * per_window)):
            two = pl.ds(w * 2 * per_window, 2 * per_window)
            s = dot_nt(k_ref[two, head(h)], q_ref[two, head(h)])
            parts.append(jnp.where(left, s[:per_window], s[per_window:]))
        local_s = jnp.concatenate(parts, axis=1)
        top = jnp.maximum(jnp.max(local_s, axis=0, keepdims=True), jnp.max(far_s, axis=0, keepdims=True))
        local_w = jnp.exp2((local_s - top) * SCALE)
        far_w = jnp.exp2((far_s - top) * SCALE)
        total = jnp.sum(local_w, axis=0, keepdims=True) + jnp.sum(far_w, axis=0, keepdims=True)
        acc = dot_tn(far_v, far_w.astype(BF16))
        parts = []
        for w in range(tokens // (2 * per_window)):
            two = pl.ds(w * 2 * per_window, 2 * per_window)
            p = local_w[:, w * 2 * per_window : (w + 1) * 2 * per_window]
            p = jnp.concatenate([jnp.where(left, p, 0.0), jnp.where(left, 0.0, p)], axis=0).astype(BF16)
            parts.append(dot_tn(v_ref[two, head(h)], p))
        acc_ref[head(h), :] = acc + jnp.concatenate(parts, axis=1)
        m_ref[h : h + 1, :] = top
        l_ref[h : h + 1, :] = total


def far_step(h, q_ref, far_ref, bias, frames, m, l, acc):
    cols = HEADS * HD
    s = dot_nt(
        jnp.concatenate([far_ref[:, head(h)], bias], axis=1),
        jnp.concatenate([q_ref[:, head(h)], frames], axis=1),
    )
    top = jnp.maximum(m, jnp.max(s, axis=0, keepdims=True))
    w = jnp.exp2((s - top) * SCALE)
    keep = jnp.exp2((m - top) * SCALE)
    l = l * keep + jnp.sum(w, axis=0, keepdims=True)
    acc = acc * keep + dot_tn(far_ref[:, head(h, cols)], w.astype(BF16))
    return top, l, acc


def middle_kernel(masks, time_ref, q_ref, far_ref, acc_in, m_in, l_in, acc_ref, m_ref, l_ref):
    tokens = q_ref.shape[0]
    bias = mask_columns(time_ref, masks, tokens // TOKENS)
    frames = frame_columns(tokens)
    for h in range(HEADS):
        m, l, acc = far_step(
            h, q_ref, far_ref, bias, frames, m_in[h : h + 1, :], l_in[h : h + 1, :], acc_in[head(h), :]
        )
        acc_ref[head(h), :] = acc
        m_ref[h : h + 1, :] = m
        l_ref[h : h + 1, :] = l


def last_kernel(masks, time_ref, q_ref, far_ref, acc_in, m_in, l_in, wo_ref, out_ref, mixed, rows_buf):
    tokens = q_ref.shape[0]
    bias = mask_columns(time_ref, masks, tokens // TOKENS)
    frames = frame_columns(tokens)
    for h in range(HEADS):
        m, l, acc = far_step(
            h, q_ref, far_ref, bias, frames, m_in[h : h + 1, :], l_in[h : h + 1, :], acc_in[head(h), :]
        )
        mixed[:, head(h)] = jnp.transpose(acc * (1.0 / l))
    per_window = WIN * WIN
    for row in range(tokens // WW):
        frame, rest = divmod(row, HH)
        wr, r = divmod(rest, WIN)
        base = frame * TOKENS + wr * (WW // WIN) * per_window + r * WIN
        line = jnp.concatenate([mixed[pl.ds(base + wc * per_window, WIN), :] for wc in range(WW // WIN)], axis=0)
        rows_buf[pl.ds(row * WW, WW), :] = line.astype(BF16)
    out_ref[...] = jnp.dot(rows_buf[...], wo_ref[...], preferred_element_type=F32).astype(BF16)


def on_device(n, frames_in, frame_time, norm_gain, w_query, w_key, w_value, w_output):
    rows = frames_in.shape[0]
    cols = HEADS * HD
    phases, held = exchange_plan(n)
    normed, block = norm_and_pool(frames_in, norm_gain, w_key, w_value)
    block, w_query, w_key, w_value = lax.optimization_barrier((block, w_query, w_key, w_value))

    def send(x, pair):
        return lax.ppermute(x, "tm", [(i, i ^ pair[i % 2]) for i in range(n)])

    projected = []
    weights = [w_query, w_key, w_value]
    share = -(-len(weights) // max(len(phases) - 1, 1))
    for i, pair in enumerate(phases[:-1]):
        block = jnp.concatenate([block, send(block, pair)], axis=0)
        take = 1 if i == 0 else share
        done = [jnp.dot(normed, w, preferred_element_type=F32).astype(BF16) for w in weights[:take]]
        weights = weights[take:]
        block, *done = lax.optimization_barrier((block, *done))
        projected += done
    projected += [jnp.dot(normed, w, preferred_element_type=F32).astype(BF16) for w in weights]
    query, keys, values = projected
    late = send(block, phases[-1])
    other = send(block, (1, 1))
    half = len(held[0]) // 2
    own = list(zip(held[0], held[1]))
    far = [(a ^ 1, b ^ 1) for b, a in own]

    state = (
        jax.ShapeDtypeStruct((cols, rows), F32),
        jax.ShapeDtypeStruct((8, rows), F32),
        jax.ShapeDtypeStruct((8, rows), F32),
    )
    params = pltpu.CompilerParams(vmem_limit_bytes=32 << 20)
    acc, m, l = pl.pallas_call(
        functools.partial(first_kernel, own[:half] + far[:half]),
        out_shape=state,
        in_specs=[SMEM] + [VMEM] * 5,
        out_specs=(VMEM, VMEM, VMEM),
        compiler_params=params,
        cost_estimate=pl.CostEstimate(flops=900_000_000, bytes_accessed=5_000_000, transcendentals=1_000_000),
        name="local_and_first",
    )(frame_time, query, keys, values, block, other)
    late, acc, m, l = lax.optimization_barrier((late, acc, m, l))
    other_late = send(late, (1, 1))
    acc, m, l = pl.pallas_call(
        functools.partial(middle_kernel, own[half:]),
        out_shape=state,
        in_specs=[SMEM] + [VMEM] * 5,
        out_specs=(VMEM, VMEM, VMEM),
        input_output_aliases={3: 0, 4: 1, 5: 2},
        compiler_params=params,
        cost_estimate=pl.CostEstimate(flops=500_000_000, bytes_accessed=5_000_000, transcendentals=400_000),
        name="middle",
    )(frame_time, query, late, acc, m, l)
    return pl.pallas_call(
        functools.partial(last_kernel, far[half:]),
        out_shape=jax.ShapeDtypeStruct((rows, w_output.shape[1]), BF16),
        in_specs=[SMEM] + [VMEM] * 6,
        out_specs=VMEM,
        scratch_shapes=[pltpu.VMEM((rows, cols), F32), pltpu.VMEM((rows, cols), BF16)],
        compiler_params=params,
        cost_estimate=pl.CostEstimate(flops=1_700_000_000, bytes_accessed=8_000_000, transcendentals=400_000),
        name="last_and_output",
    )(frame_time, query, other_late, acc, m, l, w_output)


def solution(mesh):
    placed = (P(("grp", "tm"), None), P("grp"), P(), P(), P(), P(), P())
    return jax.shard_map(
        functools.partial(on_device, mesh.shape["tm"]),
        mesh=mesh,
        in_specs=placed,
        out_specs=P(("grp", "tm"), None),
        check_vma=False,
    )
```

```python
import functools
import math

import jax
import jax.numpy as jnp
from jax import lax
from jax.experimental import pallas as pl
from jax.experimental.pallas import tpu as pltpu
from jax.sharding import PartitionSpec as P

HEADS = 6
HD = 128
HH = 16
WW = 16
WIN = 8
POOL = 4
TOKENS = HH * WW
SLOTS = TOKENS // (POOL * POOL)
FAR = -1e30
SCALE = HD**-0.5 * math.log2(math.e)
F32 = jnp.float32
BF16 = jnp.bfloat16
VMEM = pl.BlockSpec(memory_space=pltpu.VMEM)
SMEM = pl.BlockSpec(memory_space=pltpu.SMEM)
HBM = pl.BlockSpec(memory_space=pl.ANY)


def exchange_plan(n):
    high = [1 << b for b in range(n.bit_length() - 2, 0, -1)]
    first = [high[0]] + high[2:] + high[1:2]
    second = high[1:2] + high[:1] + high[2:]
    held = [[0], [0]]
    for a, b in zip(first, second):
        held = [held[0] + [m ^ a for m in held[0]], held[1] + [m ^ b for m in held[1]]]
    return list(zip(first, second)), held


def norm_kernel(
    frames_hbm, gain_hbm, wk_hbm, wv_hbm, normed_ref, pooled_ref, x_buf, gain_buf, wk_buf, wv_buf, x_sem, g_sem, w_sem
):
    rows, width = x_buf.shape
    parts = x_sem.shape[0]
    step = rows // parts
    gain_load = pltpu.make_async_copy(gain_hbm, gain_buf.at[0], g_sem)
    loads = [
        pltpu.make_async_copy(frames_hbm.at[pl.ds(i * step, step)], x_buf.at[pl.ds(i * step, step)], x_sem.at[i])
        for i in range(parts)
    ]
    weights = [
        pltpu.make_async_copy(wk_hbm, wk_buf, w_sem.at[0]),
        pltpu.make_async_copy(wv_hbm, wv_buf, w_sem.at[1]),
    ]
    for copy in loads:
        copy.start()
    gain_load.start()
    weights[0].start()
    pair = 2 * WW
    per_window = WIN * WIN
    for i in range(parts):
        loads[i].wait()
        if i == 0:
            weights[1].start()
            gain_load.wait()
            gain = gain_buf[...]
        for g in range(i * step // pair, (i + 1) * step // pair):
            x = x_buf[pl.ds(g * pair, pair), :].astype(F32)
            scale = lax.rsqrt(jnp.mean(x * x, axis=-1, keepdims=True) + 1e-06)
            y = x * scale * gain
            frame, row = divmod(2 * g, HH)
            wr, r = divmod(row, WIN)
            for wc in range(WW // WIN):
                both = jnp.concatenate(
                    [y[wc * WIN : (wc + 1) * WIN], y[WW + wc * WIN : WW + (wc + 1) * WIN]], axis=0
                )
                base = frame * TOKENS + (wr * (WW // WIN) + wc) * per_window + r * WIN
                normed_ref[pl.ds(base, 2 * WIN), :] = both.astype(BF16)
    count = rows // TOKENS
    out_rows = count * SLOTS
    slot = lax.broadcasted_iota(jnp.int32, (out_rows, rows), 0)
    token = lax.broadcasted_iota(jnp.int32, (out_rows, rows), 1)
    r, c = token % per_window // WIN, token % WIN
    home = token // per_window * 4 + r // POOL * 2 + c // POOL
    pick = jnp.where(home == slot, 1.0 / (POOL * POOL), 0.0).astype(BF16)
    mean = jnp.dot(pick, normed_ref[...], preferred_element_type=F32)
    high = mean.astype(BF16)
    low = (mean - high.astype(F32)).astype(BF16)
    both = jnp.concatenate([high, low], axis=0)
    cols = HEADS * HD
    for i, buf in enumerate((wk_buf, wv_buf)):
        weights[i].wait()
        z = jnp.dot(both, buf[...], preferred_element_type=F32)
        pooled_ref[:, i * cols : (i + 1) * cols] = (z[:out_rows] + z[out_rows:]).astype(BF16)


def norm_and_pool(frames, gain, w_key, w_value):
    rows, width = frames.shape
    out_rows = rows // TOKENS * SLOTS
    cols = HEADS * HD
    return pl.pallas_call(
        norm_kernel,
        out_shape=(
            jax.ShapeDtypeStruct((rows, width), BF16),
            jax.ShapeDtypeStruct((out_rows, 2 * cols), BF16),
        ),
        in_specs=[HBM] * 4,
        out_specs=(VMEM, VMEM),
        scratch_shapes=[
            pltpu.VMEM((rows, width), BF16),
            pltpu.VMEM((1, width), F32),
            pltpu.VMEM((width, cols), BF16),
            pltpu.VMEM((width, cols), BF16),
            pltpu.SemaphoreType.DMA((2,)),
            pltpu.SemaphoreType.DMA,
            pltpu.SemaphoreType.DMA((2,)),
        ],
        compiler_params=pltpu.CompilerParams(vmem_limit_bytes=24 << 20),
        cost_estimate=pl.CostEstimate(flops=400_000_000, bytes_accessed=8_000_000, transcendentals=0),
        name="norm_and_pool",
    )(*(pltpu.with_memory_space_constraint(x, pltpu.HBM) for x in (frames, gain, w_key, w_value)))


def own_block(me, mask_pair):
    a, b = mask_pair
    return me ^ (a if a == b else jnp.where(me % 2 == 0, a, b))


def mask_columns(time_ref, masks, count):
    me = lax.axis_index("tm")
    lane = lax.broadcasted_iota(jnp.int32, (SLOTS, HD), 1)
    own = [time_ref[me * count + f] for f in range(count)]
    tiles = []
    for pair in masks:
        source = own_block(me, pair)
        for g in range(count):
            t = time_ref[source * count + g]
            tile = jnp.zeros((SLOTS, HD), F32)
            for f in range(count):
                tile = jnp.where(lane == f, jnp.where(t < own[f], 0.0, FAR), tile)
            tiles.append(tile)
    return jnp.concatenate(tiles, axis=0).astype(BF16)


def frame_columns(tokens):
    frame = lax.broadcasted_iota(jnp.int32, (tokens, HD), 0) // TOKENS
    lane = lax.broadcasted_iota(jnp.int32, (tokens, HD), 1)
    return jnp.where(frame == lane, 1.0, 0.0).astype(BF16)


def dot_nt(a, b):
    return lax.dot_general(a, b, (((1,), (1,)), ((), ())), preferred_element_type=F32)


def dot_tn(a, b):
    return lax.dot_general(a, b, (((0,), (0,)), ((), ())), preferred_element_type=F32)


def head(h, base=0):
    return slice(base + h * HD, base + (h + 1) * HD)


def first_kernel(masks, time_ref, q_ref, k_ref, v_ref, near_ref, other_ref, acc_ref, m_ref, l_ref):
    tokens = q_ref.shape[0]
    per_window = WIN * WIN
    cols = HEADS * HD
    bias = mask_columns(time_ref, masks, tokens // TOKENS)
    frames = frame_columns(tokens)
    left = lax.broadcasted_iota(jnp.int32, (per_window, 2 * per_window), 1) < per_window
    pairs = [slice(w, w + 2 * per_window) for w in range(0, tokens, 2 * per_window)]

    def scores(h):
        q = q_ref[:, head(h)]
        far_k = jnp.concatenate([near_ref[:, head(h)], other_ref[:, head(h)]], axis=0)
        far_s = dot_nt(jnp.concatenate([far_k, bias], axis=1), jnp.concatenate([q, frames], axis=1))
        parts = []
        for two in pairs:
            s = dot_nt(k_ref[two, head(h)], q_ref[two, head(h)])
            parts.append(jnp.where(left, s[:per_window], s[per_window:]))
        return jnp.concatenate(parts, axis=1), far_s

    def weigh(h, local_s, far_s):
        top = jnp.maximum(jnp.max(local_s, axis=0, keepdims=True), jnp.max(far_s, axis=0, keepdims=True))
        local_w = jnp.exp2((local_s - top) * SCALE)
        far_w = jnp.exp2((far_s - top) * SCALE)
        m_ref[h : h + 1, :] = top
        l_ref[h : h + 1, :] = jnp.sum(local_w, axis=0, keepdims=True) + jnp.sum(far_w, axis=0, keepdims=True)
        return local_w, far_w.astype(BF16)

    def mix(h, local_w, far_w):
        far_v = jnp.concatenate([near_ref[:, head(h, cols)], other_ref[:, head(h, cols)]], axis=0)
        acc = dot_tn(far_v, far_w)
        for two in pairs:
            p = local_w[:, two]
            p = jnp.concatenate([jnp.where(left, p, 0.0), jnp.where(left, 0.0, p)], axis=0).astype(BF16)
            acc_ref[head(h), two] = acc[:, two] + dot_tn(v_ref[two, head(h)], p)

    pipelined(scores, weigh, mix)


def pipelined(scores, weigh, mix):
    ahead = 2
    ready = {h: scores(h) for h in range(ahead)}
    weights = {}
    for h in range(HEADS):
        if h + ahead < HEADS:
            ready[h + ahead] = scores(h + ahead)
        weights[h] = weigh(h, *ready.pop(h))
        if h > 0:
            mix(h - 1, *weights.pop(h - 1))
    mix(HEADS - 1, *weights.pop(HEADS - 1))


def far_stages(masks, time_ref, q_ref, far_ref, m_in, l_in, acc_in, keep_state, keep_acc):
    tokens = q_ref.shape[0]
    cols = HEADS * HD
    bias = mask_columns(time_ref, masks, tokens // TOKENS)
    frames = frame_columns(tokens)

    def scores(h):
        far_k = jnp.concatenate([far_ref[:, head(h)], bias], axis=1)
        return (dot_nt(far_k, jnp.concatenate([q_ref[:, head(h)], frames], axis=1)),)

    def weigh(h, s):
        m, l = m_in[h : h + 1, :], l_in[h : h + 1, :]
        top = jnp.maximum(m, jnp.max(s, axis=0, keepdims=True))
        w = jnp.exp2((s - top) * SCALE)
        keep = jnp.exp2((m - top) * SCALE)
        total = l * keep + jnp.sum(w, axis=0, keepdims=True)
        return w.astype(BF16), keep, keep_state(h, top, total)

    def mix(h, w, keep, state):
        keep_acc(h, acc_in[head(h), :] * keep + dot_tn(far_ref[:, head(h, cols)], w), state)

    pipelined(scores, weigh, mix)


def middle_kernel(masks, time_ref, q_ref, far_ref, acc_in, m_in, l_in, acc_ref, m_ref, l_ref):
    def keep_state(h, top, total):
        m_ref[h : h + 1, :] = top
        l_ref[h : h + 1, :] = total

    def keep_acc(h, acc, _):
        acc_ref[head(h), :] = acc

    far_stages(masks, time_ref, q_ref, far_ref, m_in, l_in, acc_in, keep_state, keep_acc)


def last_kernel(
    masks, time_ref, q_ref, far_ref, acc_in, m_in, l_in, wo_ref, out_hbm, rows_buf, out_buf, out_sem
):
    tokens = q_ref.shape[0]
    per_window = WIN * WIN

    def keep_acc(h, acc, inverse):
        mixed = jnp.transpose(acc * inverse)
        for row in range(tokens // WW):
            frame, rest = divmod(row, HH)
            wr, r = divmod(rest, WIN)
            base = frame * TOKENS + wr * (WW // WIN) * per_window + r * WIN
            starts = [base + wc * per_window for wc in range(WW // WIN)]
            line = jnp.concatenate([mixed[i : i + WIN] for i in starts], axis=0)
            rows_buf[pl.ds(row * WW, WW), head(h)] = line.astype(BF16)

    far_stages(
        masks, time_ref, q_ref, far_ref, m_in, l_in, acc_in, lambda h, top, total: 1.0 / total, keep_acc
    )
    chunks = out_sem.shape[0]
    width = out_buf.shape[1] // chunks
    copies = []
    for c in range(chunks):
        part = pl.ds(c * width, width)
        out_buf[:, part] = jnp.dot(rows_buf[...], wo_ref[:, part], preferred_element_type=F32).astype(BF16)
        copies.append(pltpu.make_async_copy(out_buf.at[:, part], out_hbm.at[:, part], out_sem.at[c]))
        copies[-1].start()
    for copy in copies:
        copy.wait()


def on_device(n, frames_in, frame_time, norm_gain, w_query, w_key, w_value, w_output):
    rows = frames_in.shape[0]
    cols = HEADS * HD
    phases, held = exchange_plan(n)
    normed, block = norm_and_pool(frames_in, norm_gain, w_key, w_value)
    block, w_query, w_key, w_value = lax.optimization_barrier((block, w_query, w_key, w_value))

    def send(x, pair):
        return lax.ppermute(x, "tm", [(i, i ^ pair[i % 2]) for i in range(n)])

    projected = []
    weights = [w_query, w_key, w_value]
    share = -(-len(weights) // max(len(phases) - 1, 1))
    for i, pair in enumerate(phases[:-1]):
        block = jnp.concatenate([block, send(block, pair)], axis=0)
        take = 1 if i == 0 else share
        done = [jnp.dot(normed, w, preferred_element_type=F32).astype(BF16) for w in weights[:take]]
        weights = weights[take:]
        block, *done = lax.optimization_barrier((block, *done))
        projected += done
    projected += [jnp.dot(normed, w, preferred_element_type=F32).astype(BF16) for w in weights]
    query, keys, values = projected
    late = send(block, phases[-1])
    other = send(block, (1, 1))
    half = len(held[0]) // 2
    own = list(zip(held[0], held[1]))
    far = [(a ^ 1, b ^ 1) for b, a in own]

    state = (
        jax.ShapeDtypeStruct((cols, rows), F32),
        jax.ShapeDtypeStruct((8, rows), F32),
        jax.ShapeDtypeStruct((8, rows), F32),
    )
    params = pltpu.CompilerParams(vmem_limit_bytes=32 << 20)
    acc, m, l = pl.pallas_call(
        functools.partial(first_kernel, own[:half] + far[:half]),
        out_shape=state,
        in_specs=[SMEM] + [VMEM] * 5,
        out_specs=(VMEM, VMEM, VMEM),
        compiler_params=params,
        cost_estimate=pl.CostEstimate(flops=900_000_000, bytes_accessed=5_000_000, transcendentals=1_000_000),
        name="local_and_first",
    )(frame_time, query, keys, values, block, other)
    late, acc, m, l = lax.optimization_barrier((late, acc, m, l))
    other_late = send(late, (1, 1))
    acc, m, l = pl.pallas_call(
        functools.partial(middle_kernel, own[half:]),
        out_shape=state,
        in_specs=[SMEM] + [VMEM] * 5,
        out_specs=(VMEM, VMEM, VMEM),
        input_output_aliases={3: 0, 4: 1, 5: 2},
        compiler_params=params,
        cost_estimate=pl.CostEstimate(flops=500_000_000, bytes_accessed=5_000_000, transcendentals=400_000),
        name="middle",
    )(frame_time, query, late, acc, m, l)
    return pl.pallas_call(
        functools.partial(last_kernel, far[half:]),
        out_shape=jax.ShapeDtypeStruct((rows, w_output.shape[1]), BF16),
        in_specs=[SMEM] + [VMEM] * 6,
        out_specs=HBM,
        scratch_shapes=[
            pltpu.VMEM((rows, cols), BF16),
            pltpu.VMEM((rows, w_output.shape[1]), BF16),
            pltpu.SemaphoreType.DMA((3,)),
        ],
        compiler_params=params,
        cost_estimate=pl.CostEstimate(flops=1_700_000_000, bytes_accessed=8_000_000, transcendentals=400_000),
        name="last_and_output",
    )(frame_time, query, other_late, acc, m, l, w_output)


def solution(mesh):
    placed = (P(("grp", "tm"), None), P("grp"), P(), P(), P(), P(), P())
    return jax.shard_map(
        functools.partial(on_device, mesh.shape["tm"]),
        mesh=mesh,
        in_specs=placed,
        out_specs=P(("grp", "tm"), None),
        check_vma=False,
    )
```

```python
import functools
import math

import jax
import jax.numpy as jnp
from jax import lax
from jax.experimental import pallas as pl
from jax.experimental.pallas import tpu as pltpu
from jax.sharding import PartitionSpec as P

HEADS = 6
HD = 128
HH = 16
WW = 16
WIN = 8
POOL = 4
TOKENS = HH * WW
SLOTS = TOKENS // (POOL * POOL)
FAR = -1e30
SCALE = HD**-0.5 * math.log2(math.e)
F32 = jnp.float32
BF16 = jnp.bfloat16
VMEM = pl.BlockSpec(memory_space=pltpu.VMEM)
HBM = pl.BlockSpec(memory_space=pl.ANY)


def exchange_plan(n):
    high = [1 << b for b in range(n.bit_length() - 2, 0, -1)]
    first = [high[0]] + high[2:] + high[1:2]
    second = high[1:2] + high[:1] + high[2:]
    held = [[0], [0]]
    for a, b in zip(first, second):
        held = [held[0] + [m ^ a for m in held[0]], held[1] + [m ^ b for m in held[1]]]
    return list(zip(first, second)), held


def norm_kernel(
    mask_groups,
    frames_hbm,
    time_hbm,
    gain_hbm,
    wk_hbm,
    wv_hbm,
    normed_ref,
    pooled_ref,
    *rest,
):
    bias_refs = rest[: len(mask_groups)]
    x_buf, time_ref, gain_buf, wk_buf, wv_buf, x_sem, t_sem, g_sem, w_sem = rest[len(mask_groups) :]
    rows, width = x_buf.shape
    parts = x_sem.shape[0]
    step = rows // parts
    gain_load = pltpu.make_async_copy(gain_hbm, gain_buf.at[0], g_sem)
    time_load = pltpu.make_async_copy(time_hbm, time_ref, t_sem)
    time_load.start()
    loads = [
        pltpu.make_async_copy(frames_hbm.at[pl.ds(i * step, step)], x_buf.at[pl.ds(i * step, step)], x_sem.at[i])
        for i in range(parts)
    ]
    weights = [
        pltpu.make_async_copy(wk_hbm, wk_buf, w_sem.at[0]),
        pltpu.make_async_copy(wv_hbm, wv_buf, w_sem.at[1]),
    ]
    for copy in loads:
        copy.start()
    gain_load.start()
    weights[0].start()
    time_load.wait()
    for masks, bias_ref in zip(mask_groups, bias_refs):
        mask_columns(time_ref, masks, rows // TOKENS, bias_ref)
    pair = 2 * WW
    per_window = WIN * WIN
    for i in range(parts):
        loads[i].wait()
        if i == 0:
            weights[1].start()
            gain_load.wait()
            gain = gain_buf[...]
        for g in range(i * step // pair, (i + 1) * step // pair):
            x = x_buf[pl.ds(g * pair, pair), :].astype(F32)
            scale = lax.rsqrt(jnp.mean(x * x, axis=-1, keepdims=True) + 1e-06)
            y = x * scale * gain
            frame, row = divmod(2 * g, HH)
            wr, r = divmod(row, WIN)
            for wc in range(WW // WIN):
                both = jnp.concatenate(
                    [y[wc * WIN : (wc + 1) * WIN], y[WW + wc * WIN : WW + (wc + 1) * WIN]], axis=0
                )
                base = frame * TOKENS + (wr * (WW // WIN) + wc) * per_window + r * WIN
                normed_ref[pl.ds(base, 2 * WIN), :] = both.astype(BF16)
    count = rows // TOKENS
    out_rows = count * SLOTS
    slot = lax.broadcasted_iota(jnp.int32, (out_rows, rows), 0)
    token = lax.broadcasted_iota(jnp.int32, (out_rows, rows), 1)
    r, c = token % per_window // WIN, token % WIN
    home = token // per_window * 4 + r // POOL * 2 + c // POOL
    pick = jnp.where(home == slot, 1.0 / (POOL * POOL), 0.0).astype(BF16)
    mean = jnp.dot(pick, normed_ref[...], preferred_element_type=F32)
    high = mean.astype(BF16)
    low = (mean - high.astype(F32)).astype(BF16)
    both = jnp.concatenate([high, low], axis=0)
    cols = HEADS * HD
    for i, buf in enumerate((wk_buf, wv_buf)):
        weights[i].wait()
        z = jnp.dot(both, buf[...], preferred_element_type=F32)
        pooled_ref[:, i * cols : (i + 1) * cols] = (z[:out_rows] + z[out_rows:]).astype(BF16)


def norm_and_pool(mask_groups, frames, frame_time, gain, w_key, w_value):
    rows, width = frames.shape
    out_rows = rows // TOKENS * SLOTS
    cols = HEADS * HD
    biases = tuple(jax.ShapeDtypeStruct((len(masks) * out_rows, HD), BF16) for masks in mask_groups)
    return pl.pallas_call(
        functools.partial(norm_kernel, mask_groups),
        out_shape=(
            jax.ShapeDtypeStruct((rows, width), BF16),
            jax.ShapeDtypeStruct((out_rows, 2 * cols), BF16),
            *biases,
        ),
        in_specs=[HBM] * 5,
        out_specs=(VMEM,) * (2 + len(biases)),
        scratch_shapes=[
            pltpu.VMEM((rows, width), BF16),
            pltpu.SMEM(frame_time.shape, jnp.int32),
            pltpu.VMEM((1, width), F32),
            pltpu.VMEM((width, cols), BF16),
            pltpu.VMEM((width, cols), BF16),
            pltpu.SemaphoreType.DMA((2,)),
            pltpu.SemaphoreType.DMA,
            pltpu.SemaphoreType.DMA,
            pltpu.SemaphoreType.DMA((2,)),
        ],
        compiler_params=pltpu.CompilerParams(vmem_limit_bytes=24 << 20),
        cost_estimate=pl.CostEstimate(flops=400_000_000, bytes_accessed=8_000_000, transcendentals=0),
        name="norm_and_pool",
    )(*(pltpu.with_memory_space_constraint(x, pltpu.HBM) for x in (frames, frame_time, gain, w_key, w_value)))


def own_block(me, mask_pair):
    a, b = mask_pair
    return me ^ (a if a == b else jnp.where(me % 2 == 0, a, b))


def mask_columns(time_ref, masks, count, bias_ref):
    me = lax.axis_index("tm")
    lane = lax.broadcasted_iota(jnp.int32, (SLOTS, HD), 1)
    own = [time_ref[me * count + f] for f in range(count)]
    for i, pair in enumerate(masks):
        source = own_block(me, pair)
        for g in range(count):
            t = time_ref[source * count + g]
            tile = jnp.zeros((SLOTS, HD), F32)
            for f in range(count):
                tile = jnp.where(lane == f, jnp.where(t < own[f], 0.0, FAR), tile)
            bias_ref[pl.ds((i * count + g) * SLOTS, SLOTS), :] = tile.astype(BF16)


def frame_columns(tokens):
    frame = lax.broadcasted_iota(jnp.int32, (tokens, HD), 0) // TOKENS
    lane = lax.broadcasted_iota(jnp.int32, (tokens, HD), 1)
    return jnp.where(frame == lane, 1.0, 0.0).astype(BF16)


def dot_nt(a, b):
    return lax.dot_general(a, b, (((1,), (1,)), ((), ())), preferred_element_type=F32)


def dot_tn(a, b):
    return lax.dot_general(a, b, (((0,), (0,)), ((), ())), preferred_element_type=F32)


def head(h, base=0):
    return slice(base + h * HD, base + (h + 1) * HD)


def first_kernel(bias_ref, q_ref, k_ref, v_ref, near_ref, other_ref, acc_ref, m_ref, l_ref):
    tokens = q_ref.shape[0]
    per_window = WIN * WIN
    cols = HEADS * HD
    bias = bias_ref[...]
    frames = frame_columns(tokens)
    left = lax.broadcasted_iota(jnp.int32, (per_window, 2 * per_window), 1) < per_window
    pairs = [slice(w, w + 2 * per_window) for w in range(0, tokens, 2 * per_window)]

    def scores(h):
        q = q_ref[:, head(h)]
        far_k = jnp.concatenate([near_ref[:, head(h)], other_ref[:, head(h)]], axis=0)
        far_s = dot_nt(jnp.concatenate([far_k, bias], axis=1), jnp.concatenate([q, frames], axis=1))
        parts = []
        for two in pairs:
            s = dot_nt(k_ref[two, head(h)], q_ref[two, head(h)])
            parts.append(jnp.where(left, s[:per_window], s[per_window:]))
        return jnp.concatenate(parts, axis=1), far_s

    def weigh(h, local_s, far_s):
        top = jnp.maximum(jnp.max(local_s, axis=0, keepdims=True), jnp.max(far_s, axis=0, keepdims=True))
        local_w = jnp.exp2((local_s - top) * SCALE)
        far_w = jnp.exp2((far_s - top) * SCALE)
        m_ref[h : h + 1, :] = top
        l_ref[h : h + 1, :] = jnp.sum(local_w, axis=0, keepdims=True) + jnp.sum(far_w, axis=0, keepdims=True)
        return local_w, far_w.astype(BF16)

    def mix(h, local_w, far_w):
        far_v = jnp.concatenate([near_ref[:, head(h, cols)], other_ref[:, head(h, cols)]], axis=0)
        acc = dot_tn(far_v, far_w)
        for two in pairs:
            p = local_w[:, two]
            p = jnp.concatenate([jnp.where(left, p, 0.0), jnp.where(left, 0.0, p)], axis=0).astype(BF16)
            acc_ref[head(h), two] = acc[:, two] + dot_tn(v_ref[two, head(h)], p)

    pipelined(scores, weigh, mix)


def pipelined(scores, weigh, mix):
    ahead = 2
    ready = {h: scores(h) for h in range(ahead)}
    weights = {}
    for h in range(HEADS):
        if h + ahead < HEADS:
            ready[h + ahead] = scores(h + ahead)
        weights[h] = weigh(h, *ready.pop(h))
        if h > 0:
            mix(h - 1, *weights.pop(h - 1))
    mix(HEADS - 1, *weights.pop(HEADS - 1))


def far_stages(bias_ref, q_ref, far_ref, m_in, l_in, acc_in, keep_state, keep_acc):
    tokens = q_ref.shape[0]
    cols = HEADS * HD
    bias = bias_ref[...]
    frames = frame_columns(tokens)

    def scores(h):
        far_k = jnp.concatenate([far_ref[:, head(h)], bias], axis=1)
        return (dot_nt(far_k, jnp.concatenate([q_ref[:, head(h)], frames], axis=1)),)

    def weigh(h, s):
        m, l = m_in[h : h + 1, :], l_in[h : h + 1, :]
        top = jnp.maximum(m, jnp.max(s, axis=0, keepdims=True))
        w = jnp.exp2((s - top) * SCALE)
        keep = jnp.exp2((m - top) * SCALE)
        total = l * keep + jnp.sum(w, axis=0, keepdims=True)
        return w.astype(BF16), keep, keep_state(h, top, total)

    def mix(h, w, keep, state):
        keep_acc(h, acc_in[head(h), :] * keep + dot_tn(far_ref[:, head(h, cols)], w), state)

    pipelined(scores, weigh, mix)


def middle_kernel(bias_ref, q_ref, far_ref, acc_in, m_in, l_in, acc_ref, m_ref, l_ref):
    def keep_state(h, top, total):
        m_ref[h : h + 1, :] = top
        l_ref[h : h + 1, :] = total

    def keep_acc(h, acc, _):
        acc_ref[head(h), :] = acc

    far_stages(bias_ref, q_ref, far_ref, m_in, l_in, acc_in, keep_state, keep_acc)


def last_kernel(
    bias_ref, q_ref, far_ref, acc_in, m_in, l_in, wo_ref, out_hbm, rows_buf, out_buf, out_sem
):
    tokens = q_ref.shape[0]
    per_window = WIN * WIN

    def keep_acc(h, acc, inverse):
        mixed = jnp.transpose(acc * inverse)
        for row in range(tokens // WW):
            frame, rest = divmod(row, HH)
            wr, r = divmod(rest, WIN)
            base = frame * TOKENS + wr * (WW // WIN) * per_window + r * WIN
            starts = [base + wc * per_window for wc in range(WW // WIN)]
            line = jnp.concatenate([mixed[i : i + WIN] for i in starts], axis=0)
            rows_buf[pl.ds(row * WW, WW), head(h)] = line.astype(BF16)

    far_stages(
        bias_ref, q_ref, far_ref, m_in, l_in, acc_in, lambda h, top, total: 1.0 / total, keep_acc
    )
    chunks = out_sem.shape[0]
    width = out_buf.shape[1] // chunks
    copies = []
    for c in range(chunks):
        part = pl.ds(c * width, width)
        out_buf[:, part] = jnp.dot(rows_buf[...], wo_ref[:, part], preferred_element_type=F32).astype(BF16)
        copies.append(pltpu.make_async_copy(out_buf.at[:, part], out_hbm.at[:, part], out_sem.at[c]))
        copies[-1].start()
    for copy in copies:
        copy.wait()


def on_device(n, frames_in, frame_time, norm_gain, w_query, w_key, w_value, w_output):
    rows = frames_in.shape[0]
    cols = HEADS * HD
    phases, held = exchange_plan(n)
    half = len(held[0]) // 2
    own = list(zip(held[0], held[1]))
    far = [(a ^ 1, b ^ 1) for b, a in own]
    groups = (own[:half] + far[:half], own[half:], far[half:])
    normed, block, *bias = norm_and_pool(groups, frames_in, frame_time, norm_gain, w_key, w_value)
    block, w_query, w_key, w_value = lax.optimization_barrier((block, w_query, w_key, w_value))

    def send(x, pair):
        return lax.ppermute(x, "tm", [(i, i ^ pair[i % 2]) for i in range(n)])

    projected = []
    weights = [w_query, w_key, w_value]
    for i, pair in enumerate(phases[:-1]):
        came = send(block, pair)
        take = 1 if i == 0 else len(weights)
        done = [jnp.dot(normed, w, preferred_element_type=F32).astype(BF16) for w in weights[:take]]
        weights = weights[take:]
        block = jnp.concatenate([block, came], axis=0)
        block, normed, *done = lax.optimization_barrier((block, normed, *done))
        projected += done
    projected += [jnp.dot(normed, w, preferred_element_type=F32).astype(BF16) for w in weights]
    query, keys, values = projected
    late = send(block, phases[-1])
    other = send(block, (1, 1))

    state = (
        jax.ShapeDtypeStruct((cols, rows), F32),
        jax.ShapeDtypeStruct((8, rows), F32),
        jax.ShapeDtypeStruct((8, rows), F32),
    )
    params = pltpu.CompilerParams(vmem_limit_bytes=32 << 20)
    acc, m, l = pl.pallas_call(
        first_kernel,
        out_shape=state,
        in_specs=[VMEM] * 6,
        out_specs=(VMEM, VMEM, VMEM),
        compiler_params=params,
        cost_estimate=pl.CostEstimate(flops=900_000_000, bytes_accessed=5_000_000, transcendentals=1_000_000),
        name="local_and_first",
    )(bias[0], query, keys, values, block, other)
    late, acc, m, l = lax.optimization_barrier((late, acc, m, l))
    other_late = send(late, (1, 1))
    acc, m, l = pl.pallas_call(
        middle_kernel,
        out_shape=state,
        in_specs=[VMEM] * 6,
        out_specs=(VMEM, VMEM, VMEM),
        input_output_aliases={3: 0, 4: 1, 5: 2},
        compiler_params=params,
        cost_estimate=pl.CostEstimate(flops=500_000_000, bytes_accessed=5_000_000, transcendentals=400_000),
        name="middle",
    )(bias[1], query, late, acc, m, l)
    return pl.pallas_call(
        last_kernel,
        out_shape=jax.ShapeDtypeStruct((rows, w_output.shape[1]), BF16),
        in_specs=[VMEM] * 7,
        out_specs=HBM,
        scratch_shapes=[
            pltpu.VMEM((rows, cols), BF16),
            pltpu.VMEM((rows, w_output.shape[1]), BF16),
            pltpu.SemaphoreType.DMA((3,)),
        ],
        compiler_params=params,
        cost_estimate=pl.CostEstimate(flops=1_700_000_000, bytes_accessed=8_000_000, transcendentals=400_000),
        name="last_and_output",
    )(bias[2], query, other_late, acc, m, l, w_output)


def solution(mesh):
    placed = (P(("grp", "tm"), None), P("grp"), P(), P(), P(), P(), P())
    return jax.shard_map(
        functools.partial(on_device, mesh.shape["tm"]),
        mesh=mesh,
        in_specs=placed,
        out_specs=P(("grp", "tm"), None),
        check_vma=False,
    )
```

```python
import functools
import math

import jax
import jax.numpy as jnp
from jax import lax
from jax.experimental import pallas as pl
from jax.experimental.pallas import tpu as pltpu
from jax.sharding import PartitionSpec as P

HEADS = 6
HD = 128
HH = 16
WW = 16
WIN = 8
POOL = 4
TOKENS = HH * WW
SLOTS = TOKENS // (POOL * POOL)
FAR = -1e30
SCALE = HD**-0.5 * math.log2(math.e)
F32 = jnp.float32
BF16 = jnp.bfloat16
VMEM = pl.BlockSpec(memory_space=pltpu.VMEM)
HBM = pl.BlockSpec(memory_space=pl.ANY)


def exchange_plan(n):
    high = [1 << b for b in range(n.bit_length() - 2, 0, -1)]
    phases = list(zip(high, high[-1:] + high[:-1]))
    held = []
    for core in range(2):
        masks = [0]
        for pair in phases[:-2]:
            masks = masks + [m ^ pair[core] for m in masks]
        before, last = phases[-2][core], phases[-1][core]
        brought = [m ^ before for m in masks]
        held.append((masks + brought + [m ^ last for m in masks], [m ^ last for m in brought]))
    return phases, held


def norm_kernel(
    mask_groups,
    frames_hbm,
    time_hbm,
    gain_hbm,
    wk_hbm,
    wv_hbm,
    normed_ref,
    pooled_ref,
    *rest,
):
    bias_refs = rest[: len(mask_groups)]
    x_buf, time_ref, gain_buf, wk_buf, wv_buf, x_sem, t_sem, g_sem, w_sem = rest[len(mask_groups) :]
    rows, width = x_buf.shape
    parts = x_sem.shape[0]
    step = rows // parts
    gain_load = pltpu.make_async_copy(gain_hbm, gain_buf.at[0], g_sem)
    time_load = pltpu.make_async_copy(time_hbm, time_ref, t_sem)
    time_load.start()
    loads = [
        pltpu.make_async_copy(frames_hbm.at[pl.ds(i * step, step)], x_buf.at[pl.ds(i * step, step)], x_sem.at[i])
        for i in range(parts)
    ]
    weights = [
        pltpu.make_async_copy(wk_hbm, wk_buf, w_sem.at[0]),
        pltpu.make_async_copy(wv_hbm, wv_buf, w_sem.at[1]),
    ]
    for copy in loads:
        copy.start()
    gain_load.start()
    weights[0].start()
    time_load.wait()
    for masks, bias_ref in zip(mask_groups, bias_refs):
        mask_columns(time_ref, masks, rows // TOKENS, bias_ref)
    pair = 2 * WW
    per_window = WIN * WIN
    for i in range(parts):
        loads[i].wait()
        if i == 0:
            weights[1].start()
            gain_load.wait()
            gain = gain_buf[...]
        for g in range(i * step // pair, (i + 1) * step // pair):
            x = x_buf[pl.ds(g * pair, pair), :].astype(F32)
            scale = lax.rsqrt(jnp.mean(x * x, axis=-1, keepdims=True) + 1e-06)
            y = x * scale * gain
            frame, row = divmod(2 * g, HH)
            wr, r = divmod(row, WIN)
            for wc in range(WW // WIN):
                both = jnp.concatenate(
                    [y[wc * WIN : (wc + 1) * WIN], y[WW + wc * WIN : WW + (wc + 1) * WIN]], axis=0
                )
                base = frame * TOKENS + (wr * (WW // WIN) + wc) * per_window + r * WIN
                normed_ref[pl.ds(base, 2 * WIN), :] = both.astype(BF16)
    count = rows // TOKENS
    out_rows = count * SLOTS
    slot = lax.broadcasted_iota(jnp.int32, (out_rows, rows), 0)
    token = lax.broadcasted_iota(jnp.int32, (out_rows, rows), 1)
    r, c = token % per_window // WIN, token % WIN
    home = token // per_window * 4 + r // POOL * 2 + c // POOL
    pick = jnp.where(home == slot, 1.0 / (POOL * POOL), 0.0).astype(BF16)
    mean = jnp.dot(pick, normed_ref[...], preferred_element_type=F32)
    high = mean.astype(BF16)
    low = (mean - high.astype(F32)).astype(BF16)
    both = jnp.concatenate([high, low], axis=0)
    cols = HEADS * HD
    for i, buf in enumerate((wk_buf, wv_buf)):
        weights[i].wait()
        z = jnp.dot(both, buf[...], preferred_element_type=F32)
        pooled_ref[:, i * cols : (i + 1) * cols] = (z[:out_rows] + z[out_rows:]).astype(BF16)


def norm_and_pool(mask_groups, frames, frame_time, gain, w_key, w_value):
    rows, width = frames.shape
    out_rows = rows // TOKENS * SLOTS
    cols = HEADS * HD
    biases = tuple(jax.ShapeDtypeStruct((len(masks) * out_rows, HD), BF16) for masks in mask_groups)
    return pl.pallas_call(
        functools.partial(norm_kernel, mask_groups),
        out_shape=(
            jax.ShapeDtypeStruct((rows, width), BF16),
            jax.ShapeDtypeStruct((out_rows, 2 * cols), BF16),
            *biases,
        ),
        in_specs=[HBM] * 5,
        out_specs=(VMEM,) * (2 + len(biases)),
        scratch_shapes=[
            pltpu.VMEM((rows, width), BF16),
            pltpu.SMEM(frame_time.shape, jnp.int32),
            pltpu.VMEM((1, width), F32),
            pltpu.VMEM((width, cols), BF16),
            pltpu.VMEM((width, cols), BF16),
            pltpu.SemaphoreType.DMA((2,)),
            pltpu.SemaphoreType.DMA,
            pltpu.SemaphoreType.DMA,
            pltpu.SemaphoreType.DMA((2,)),
        ],
        compiler_params=pltpu.CompilerParams(vmem_limit_bytes=24 << 20),
        cost_estimate=pl.CostEstimate(flops=400_000_000, bytes_accessed=8_000_000, transcendentals=0),
        name="norm_and_pool",
    )(*(pltpu.with_memory_space_constraint(x, pltpu.HBM) for x in (frames, frame_time, gain, w_key, w_value)))


def own_block(me, mask_pair):
    a, b = mask_pair
    return me ^ (a if a == b else jnp.where(me % 2 == 0, a, b))


def mask_columns(time_ref, masks, count, bias_ref):
    me = lax.axis_index("tm")
    lane = lax.broadcasted_iota(jnp.int32, (SLOTS, HD), 1)
    own = [time_ref[me * count + f] for f in range(count)]
    for i, pair in enumerate(masks):
        source = own_block(me, pair)
        for g in range(count):
            t = time_ref[source * count + g]
            tile = jnp.zeros((SLOTS, HD), F32)
            for f in range(count):
                tile = jnp.where(lane == f, jnp.where(t < own[f], 0.0, FAR), tile)
            bias_ref[pl.ds((i * count + g) * SLOTS, SLOTS), :] = tile.astype(BF16)


def frame_columns(tokens):
    frame = lax.broadcasted_iota(jnp.int32, (tokens, HD), 0) // TOKENS
    lane = lax.broadcasted_iota(jnp.int32, (tokens, HD), 1)
    return jnp.where(frame == lane, 1.0, 0.0).astype(BF16)


def dot_nt(a, b):
    return lax.dot_general(a, b, (((1,), (1,)), ((), ())), preferred_element_type=F32)


def dot_tn(a, b):
    return lax.dot_general(a, b, (((0,), (0,)), ((), ())), preferred_element_type=F32)


def head(h, base=0):
    return slice(base + h * HD, base + (h + 1) * HD)


def first_kernel(bias_ref, q_ref, k_ref, v_ref, near_ref, other_ref, acc_ref, m_ref, l_ref):
    tokens = q_ref.shape[0]
    per_window = WIN * WIN
    cols = HEADS * HD
    bias = bias_ref[...]
    frames = frame_columns(tokens)
    left = lax.broadcasted_iota(jnp.int32, (per_window, 2 * per_window), 1) < per_window
    pairs = [slice(w, w + 2 * per_window) for w in range(0, tokens, 2 * per_window)]

    def scores(h):
        q = q_ref[:, head(h)]
        far_k = jnp.concatenate([near_ref[:, head(h)], other_ref[:, head(h)]], axis=0)
        far_s = dot_nt(jnp.concatenate([far_k, bias], axis=1), jnp.concatenate([q, frames], axis=1))
        parts = []
        for two in pairs:
            s = dot_nt(k_ref[two, head(h)], q_ref[two, head(h)])
            parts.append(jnp.where(left, s[:per_window], s[per_window:]))
        return jnp.concatenate(parts, axis=1), far_s

    def weigh(h, local_s, far_s):
        top = jnp.maximum(jnp.max(local_s, axis=0, keepdims=True), jnp.max(far_s, axis=0, keepdims=True))
        local_w = jnp.exp2((local_s - top) * SCALE)
        far_w = jnp.exp2((far_s - top) * SCALE)
        m_ref[h : h + 1, :] = top
        l_ref[h : h + 1, :] = jnp.sum(local_w, axis=0, keepdims=True) + jnp.sum(far_w, axis=0, keepdims=True)
        return local_w, far_w.astype(BF16)

    def mix(h, local_w, far_w):
        far_v = jnp.concatenate([near_ref[:, head(h, cols)], other_ref[:, head(h, cols)]], axis=0)
        acc = dot_tn(far_v, far_w)
        for two in pairs:
            p = local_w[:, two]
            p = jnp.concatenate([jnp.where(left, p, 0.0), jnp.where(left, 0.0, p)], axis=0).astype(BF16)
            acc_ref[head(h), two] = acc[:, two] + dot_tn(v_ref[two, head(h)], p)

    pipelined(scores, weigh, mix)


def pipelined(scores, weigh, mix):
    ahead = 2
    ready = {h: scores(h) for h in range(ahead)}
    weights = {}
    for h in range(HEADS):
        if h + ahead < HEADS:
            ready[h + ahead] = scores(h + ahead)
        weights[h] = weigh(h, *ready.pop(h))
        if h > 0:
            mix(h - 1, *weights.pop(h - 1))
    mix(HEADS - 1, *weights.pop(HEADS - 1))


def far_stages(bias_ref, q_ref, far_ref, m_in, l_in, acc_in, keep_state, keep_acc):
    tokens = q_ref.shape[0]
    cols = HEADS * HD
    bias = bias_ref[...]
    frames = frame_columns(tokens)

    def scores(h):
        far_k = jnp.concatenate([far_ref[:, head(h)], bias], axis=1)
        return (dot_nt(far_k, jnp.concatenate([q_ref[:, head(h)], frames], axis=1)),)

    def weigh(h, s):
        m, l = m_in[h : h + 1, :], l_in[h : h + 1, :]
        top = jnp.maximum(m, jnp.max(s, axis=0, keepdims=True))
        w = jnp.exp2((s - top) * SCALE)
        keep = jnp.exp2((m - top) * SCALE)
        total = l * keep + jnp.sum(w, axis=0, keepdims=True)
        return w.astype(BF16), keep, keep_state(h, top, total)

    def mix(h, w, keep, state):
        keep_acc(h, acc_in[head(h), :] * keep + dot_tn(far_ref[:, head(h, cols)], w), state)

    pipelined(scores, weigh, mix)


def middle_kernel(bias_ref, q_ref, far_ref, acc_in, m_in, l_in, acc_ref, m_ref, l_ref):
    def keep_state(h, top, total):
        m_ref[h : h + 1, :] = top
        l_ref[h : h + 1, :] = total

    def keep_acc(h, acc, _):
        acc_ref[head(h), :] = acc

    far_stages(bias_ref, q_ref, far_ref, m_in, l_in, acc_in, keep_state, keep_acc)


def last_kernel(
    bias_ref, q_ref, far_ref, acc_in, m_in, l_in, wo_ref, out_hbm, rows_buf, out_buf, out_sem
):
    tokens = q_ref.shape[0]
    per_window = WIN * WIN

    def keep_acc(h, acc, inverse):
        mixed = jnp.transpose(acc * inverse)
        for row in range(tokens // WW):
            frame, rest = divmod(row, HH)
            wr, r = divmod(rest, WIN)
            base = frame * TOKENS + wr * (WW // WIN) * per_window + r * WIN
            starts = [base + wc * per_window for wc in range(WW // WIN)]
            line = jnp.concatenate([mixed[i : i + WIN] for i in starts], axis=0)
            rows_buf[pl.ds(row * WW, WW), head(h)] = line.astype(BF16)

    far_stages(
        bias_ref, q_ref, far_ref, m_in, l_in, acc_in, lambda h, top, total: 1.0 / total, keep_acc
    )
    chunks = out_sem.shape[0]
    width = out_buf.shape[1] // chunks
    copies = []
    for c in range(chunks):
        part = pl.ds(c * width, width)
        out_buf[:, part] = jnp.dot(rows_buf[...], wo_ref[:, part], preferred_element_type=F32).astype(BF16)
        copies.append(pltpu.make_async_copy(out_buf.at[:, part], out_hbm.at[:, part], out_sem.at[c]))
        copies[-1].start()
    for copy in copies:
        copy.wait()


def on_device(n, frames_in, frame_time, norm_gain, w_query, w_key, w_value, w_output):
    rows = frames_in.shape[0]
    cols = HEADS * HD
    phases, held = exchange_plan(n)
    own, own_late = (list(zip(x, y)) for x, y in zip(*held))
    far, far_late = ([(y ^ 1, x ^ 1) for x, y in masks] for masks in (own, own_late))
    groups = (own + far, own_late, far_late)
    normed, block, *bias = norm_and_pool(groups, frames_in, frame_time, norm_gain, w_key, w_value)
    block, w_query, w_key, w_value = lax.optimization_barrier((block, w_query, w_key, w_value))

    def send(x, pair):
        return lax.ppermute(x, "tm", [(i, i ^ pair[i % 2]) for i in range(n)])

    def project(w):
        return jnp.dot(normed, w, preferred_element_type=F32).astype(BF16)

    query = None
    for pair in phases[:-2]:
        came = send(block, pair)
        query = project(w_query) if query is None else query
        block = jnp.concatenate([block, came], axis=0)
        block, normed, query = lax.optimization_barrier((block, normed, query))
    brought = send(block, phases[-2])
    early = send(block, phases[-1])
    keys, values = project(w_key), project(w_value)
    brought, early, keys, values = lax.optimization_barrier((brought, early, keys, values))
    late = send(brought, phases[-1])
    block = jnp.concatenate([block, brought, early], axis=0)
    other = send(block, (1, 1))
    state = (
        jax.ShapeDtypeStruct((cols, rows), F32),
        jax.ShapeDtypeStruct((8, rows), F32),
        jax.ShapeDtypeStruct((8, rows), F32),
    )
    params = pltpu.CompilerParams(vmem_limit_bytes=32 << 20)
    acc, m, l = pl.pallas_call(
        first_kernel,
        out_shape=state,
        in_specs=[VMEM] * 6,
        out_specs=(VMEM, VMEM, VMEM),
        compiler_params=params,
        cost_estimate=pl.CostEstimate(flops=900_000_000, bytes_accessed=5_000_000, transcendentals=1_000_000),
        name="local_and_first",
    )(bias[0], query, keys, values, block, other)
    late, acc, m, l = lax.optimization_barrier((late, acc, m, l))
    other_late = send(late, (1, 1))
    acc, m, l = pl.pallas_call(
        middle_kernel,
        out_shape=state,
        in_specs=[VMEM] * 6,
        out_specs=(VMEM, VMEM, VMEM),
        input_output_aliases={3: 0, 4: 1, 5: 2},
        compiler_params=params,
        cost_estimate=pl.CostEstimate(flops=500_000_000, bytes_accessed=5_000_000, transcendentals=400_000),
        name="middle",
    )(bias[1], query, late, acc, m, l)
    return pl.pallas_call(
        last_kernel,
        out_shape=jax.ShapeDtypeStruct((rows, w_output.shape[1]), BF16),
        in_specs=[VMEM] * 7,
        out_specs=HBM,
        scratch_shapes=[
            pltpu.VMEM((rows, cols), BF16),
            pltpu.VMEM((rows, w_output.shape[1]), BF16),
            pltpu.SemaphoreType.DMA((3,)),
        ],
        compiler_params=params,
        cost_estimate=pl.CostEstimate(flops=1_700_000_000, bytes_accessed=8_000_000, transcendentals=400_000),
        name="last_and_output",
    )(bias[2], query, other_late, acc, m, l, w_output)


def solution(mesh):
    placed = (P(("grp", "tm"), None), P("grp"), P(), P(), P(), P(), P())
    return jax.shard_map(
        functools.partial(on_device, mesh.shape["tm"]),
        mesh=mesh,
        in_specs=placed,
        out_specs=P(("grp", "tm"), None),
        check_vma=False,
    )
```

```python
import functools
import math

import jax
import jax.numpy as jnp
from jax import lax
from jax.experimental import pallas as pl
from jax.experimental.pallas import tpu as pltpu
from jax.sharding import PartitionSpec as P

HEADS = 6
HD = 128
HH = 16
WW = 16
WIN = 8
POOL = 4
TOKENS = HH * WW
SLOTS = TOKENS // (POOL * POOL)
FAR = -1e30
SCALE = HD**-0.5 * math.log2(math.e)
F32 = jnp.float32
BF16 = jnp.bfloat16
VMEM = pl.BlockSpec(memory_space=pltpu.VMEM)
HBM = pl.BlockSpec(memory_space=pl.ANY)


def exchange_plan(n):
    high = [1 << b for b in range(n.bit_length() - 2, 0, -1)]
    phases = list(zip(high, high[-1:] + high[:-1]))
    held = []
    for core in range(2):
        masks = [0]
        for pair in phases[:-2]:
            masks = masks + [m ^ pair[core] for m in masks]
        before, last = phases[-2][core], phases[-1][core]
        brought = [m ^ before for m in masks]
        held.append((masks + brought + [m ^ last for m in masks], [m ^ last for m in brought]))
    return phases, held


def norm_kernel(mask_groups, frames_hbm, time_hbm, gain_hbm, normed_ref, high_ref, low_ref, *rest):
    bias_refs = rest[: len(mask_groups)]
    x_buf, time_ref, gain_buf, x_sem, t_sem, g_sem = rest[len(mask_groups) :]
    rows, width = x_buf.shape
    parts = x_sem.shape[0]
    step = rows // parts
    loads = [
        pltpu.make_async_copy(frames_hbm.at[pl.ds(i * step, step)], x_buf.at[pl.ds(i * step, step)], x_sem.at[i])
        for i in range(parts)
    ]
    gain_load = pltpu.make_async_copy(gain_hbm, gain_buf.at[0], g_sem)
    time_load = pltpu.make_async_copy(time_hbm, time_ref, t_sem)
    for copy in loads + [gain_load, time_load]:
        copy.start()
    gain_load.wait()
    gain = gain_buf[...]
    time_load.wait()
    for masks, bias_ref in zip(mask_groups, bias_refs):
        mask_rows(time_ref, masks, rows // TOKENS, bias_ref)
    pair = 2 * WW
    per_window = WIN * WIN
    for i in range(parts):
        loads[i].wait()
        for g in range(i * step // pair, (i + 1) * step // pair):
            x = x_buf[pl.ds(g * pair, pair), :].astype(F32)
            scale = lax.rsqrt(jnp.mean(x * x, axis=-1, keepdims=True) + 1e-06)
            y = x * scale * gain
            frame, row = divmod(2 * g, HH)
            wr, r = divmod(row, WIN)
            for wc in range(WW // WIN):
                both = jnp.concatenate(
                    [y[wc * WIN : (wc + 1) * WIN], y[WW + wc * WIN : WW + (wc + 1) * WIN]], axis=0
                )
                base = frame * TOKENS + (wr * (WW // WIN) + wc) * per_window + r * WIN
                normed_ref[pl.ds(base, 2 * WIN), :] = both.astype(BF16)
    count = rows // TOKENS
    out_rows = count * SLOTS
    slot = lax.broadcasted_iota(jnp.int32, (out_rows, rows), 0)
    token = lax.broadcasted_iota(jnp.int32, (out_rows, rows), 1)
    r, c = token % per_window // WIN, token % WIN
    home = token // per_window * 4 + r // POOL * 2 + c // POOL
    pick = jnp.where(home == slot, 1.0 / (POOL * POOL), 0.0).astype(BF16)
    mean = jnp.dot(pick, normed_ref[...], preferred_element_type=F32)
    high = mean.astype(BF16)
    high_ref[...] = high
    low_ref[...] = (mean - high.astype(F32)).astype(BF16)


def norm_and_pool(mask_groups, frames, frame_time, gain):
    rows, width = frames.shape
    count = rows // TOKENS
    pooled = jax.ShapeDtypeStruct((count * SLOTS, width), BF16)
    biases = tuple(jax.ShapeDtypeStruct((len(masks) * count * SLOTS, count * HD), F32) for masks in mask_groups)
    return pl.pallas_call(
        functools.partial(norm_kernel, mask_groups),
        out_shape=(jax.ShapeDtypeStruct((rows, width), BF16), pooled, pooled, *biases),
        in_specs=[HBM] * 3,
        out_specs=(VMEM,) * (3 + len(biases)),
        scratch_shapes=[
            pltpu.VMEM((rows, width), BF16),
            pltpu.SMEM(frame_time.shape, jnp.int32),
            pltpu.VMEM((1, width), F32),
            pltpu.SemaphoreType.DMA((2,)),
            pltpu.SemaphoreType.DMA,
            pltpu.SemaphoreType.DMA,
        ],
        compiler_params=pltpu.CompilerParams(vmem_limit_bytes=16 << 20),
        cost_estimate=pl.CostEstimate(flops=400_000_000, bytes_accessed=8_000_000, transcendentals=0),
        name="norm_and_pool",
    )(*(pltpu.with_memory_space_constraint(x, pltpu.HBM) for x in (frames, frame_time, gain)))


def pooled_kernel(high_ref, low_ref, came_ref, wk_ref, wv_ref, out_ref):
    rows = high_ref.shape[0]
    x = jnp.concatenate([high_ref[...], low_ref[...], came_ref[...]], axis=0)
    cols = HEADS * HD
    for i, w_ref in enumerate((wk_ref, wv_ref)):
        z = jnp.dot(x, w_ref[...], preferred_element_type=F32)
        part = slice(i * cols, (i + 1) * cols)
        out_ref[:, part] = jnp.concatenate([z[:rows] + z[rows : 2 * rows], z[2 * rows :]], axis=0).astype(BF16)


def own_block(me, mask_pair):
    a, b = mask_pair
    return me ^ (a if a == b else jnp.where(me % 2 == 0, a, b))


def mask_rows(time_ref, masks, count, bias_ref):
    me = lax.axis_index("tm")
    own = [time_ref[me * count + f] for f in range(count)]
    for i, pair in enumerate(masks):
        source = own_block(me, pair)
        for g in range(count):
            t = time_ref[source * count + g]
            for f in range(count):
                value = jnp.where(t < own[f], 0.0, FAR).astype(F32)
                bias_ref[pl.ds((i * count + g) * SLOTS, SLOTS), head(f)] = jnp.full((SLOTS, HD), value, F32)


def mask_scores(s, bias):
    copies = TOKENS // HD
    columns = [bias[:, head(f)] for f in range(s.shape[1] // TOKENS) for _ in range(copies)]
    return s + jnp.concatenate(columns, axis=1)


def dot_nt(a, b):
    return lax.dot_general(a, b, (((1,), (1,)), ((), ())), preferred_element_type=F32)


def dot_tn(a, b):
    return lax.dot_general(a, b, (((0,), (0,)), ((), ())), preferred_element_type=F32)


def head(h, base=0):
    return slice(base + h * HD, base + (h + 1) * HD)


def first_kernel(bias_ref, q_ref, k_ref, v_ref, near_ref, other_ref, acc_ref, m_ref, l_ref):
    tokens = q_ref.shape[0]
    per_window = WIN * WIN
    cols = HEADS * HD
    bias = bias_ref[...]
    left = lax.broadcasted_iota(jnp.int32, (per_window, 2 * per_window), 1) < per_window
    pairs = [slice(w, w + 2 * per_window) for w in range(0, tokens, 2 * per_window)]

    def scores(h):
        q = q_ref[:, head(h)]
        far_k = jnp.concatenate([near_ref[:, head(h)], other_ref[:, head(h)]], axis=0)
        far_s = mask_scores(dot_nt(far_k, q), bias)
        parts = []
        for two in pairs:
            s = dot_nt(k_ref[two, head(h)], q_ref[two, head(h)])
            parts.append(jnp.where(left, s[:per_window], s[per_window:]))
        return jnp.concatenate(parts, axis=1), far_s

    def weigh(h, local_s, far_s):
        top = jnp.maximum(jnp.max(local_s, axis=0, keepdims=True), jnp.max(far_s, axis=0, keepdims=True))
        local_w = jnp.exp2((local_s - top) * SCALE)
        far_w = jnp.exp2((far_s - top) * SCALE)
        m_ref[h : h + 1, :] = top
        l_ref[h : h + 1, :] = jnp.sum(local_w, axis=0, keepdims=True) + jnp.sum(far_w, axis=0, keepdims=True)
        return local_w, far_w.astype(BF16)

    def mix(h, local_w, far_w):
        far_v = jnp.concatenate([near_ref[:, head(h, cols)], other_ref[:, head(h, cols)]], axis=0)
        acc = dot_tn(far_v, far_w)
        for two in pairs:
            p = local_w[:, two]
            p = jnp.concatenate([jnp.where(left, p, 0.0), jnp.where(left, 0.0, p)], axis=0).astype(BF16)
            acc_ref[head(h), two] = acc[:, two] + dot_tn(v_ref[two, head(h)], p)

    pipelined(scores, weigh, mix)


def pipelined(scores, weigh, mix):
    ahead = 2
    ready = {h: scores(h) for h in range(ahead)}
    weights = {}
    for h in range(HEADS):
        if h + ahead < HEADS:
            ready[h + ahead] = scores(h + ahead)
        weights[h] = weigh(h, *ready.pop(h))
        if h > 0:
            mix(h - 1, *weights.pop(h - 1))
    mix(HEADS - 1, *weights.pop(HEADS - 1))


def far_stages(bias_ref, q_ref, far_ref, m_in, l_in, acc_in, keep_state, keep_acc):
    cols = HEADS * HD
    bias = bias_ref[...]

    def scores(h):
        return (mask_scores(dot_nt(far_ref[:, head(h)], q_ref[:, head(h)]), bias),)

    def weigh(h, s):
        m, l = m_in[h : h + 1, :], l_in[h : h + 1, :]
        top = jnp.maximum(m, jnp.max(s, axis=0, keepdims=True))
        w = jnp.exp2((s - top) * SCALE)
        keep = jnp.exp2((m - top) * SCALE)
        total = l * keep + jnp.sum(w, axis=0, keepdims=True)
        return w.astype(BF16), keep, keep_state(h, top, total)

    def mix(h, w, keep, state):
        keep_acc(h, acc_in[head(h), :] * keep + dot_tn(far_ref[:, head(h, cols)], w), state)

    pipelined(scores, weigh, mix)


def middle_kernel(bias_ref, q_ref, far_ref, acc_in, m_in, l_in, acc_ref, m_ref, l_ref):
    def keep_state(h, top, total):
        m_ref[h : h + 1, :] = top
        l_ref[h : h + 1, :] = total

    def keep_acc(h, acc, _):
        acc_ref[head(h), :] = acc

    far_stages(bias_ref, q_ref, far_ref, m_in, l_in, acc_in, keep_state, keep_acc)


def last_kernel(
    bias_ref, q_ref, far_ref, acc_in, m_in, l_in, wo_ref, out_hbm, rows_buf, out_buf, out_sem
):
    tokens = q_ref.shape[0]
    per_window = WIN * WIN

    def keep_acc(h, acc, inverse):
        mixed = jnp.transpose(acc * inverse)
        for row in range(tokens // WW):
            frame, rest = divmod(row, HH)
            wr, r = divmod(rest, WIN)
            base = frame * TOKENS + wr * (WW // WIN) * per_window + r * WIN
            starts = [base + wc * per_window for wc in range(WW // WIN)]
            line = jnp.concatenate([mixed[i : i + WIN] for i in starts], axis=0)
            rows_buf[pl.ds(row * WW, WW), head(h)] = line.astype(BF16)

    far_stages(
        bias_ref, q_ref, far_ref, m_in, l_in, acc_in, lambda h, top, total: 1.0 / total, keep_acc
    )
    chunks = out_sem.shape[0]
    width = out_buf.shape[1] // chunks
    copies = []
    for c in range(chunks):
        part = pl.ds(c * width, width)
        out_buf[:, part] = jnp.dot(rows_buf[...], wo_ref[:, part], preferred_element_type=F32).astype(BF16)
        copies.append(pltpu.make_async_copy(out_buf.at[:, part], out_hbm.at[:, part], out_sem.at[c]))
        copies[-1].start()
    for copy in copies:
        copy.wait()


def on_device(n, frames_in, frame_time, norm_gain, w_query, w_key, w_value, w_output):
    rows = frames_in.shape[0]
    cols = HEADS * HD
    phases, held = exchange_plan(n)
    own, own_late = (list(zip(x, y)) for x, y in zip(*held))
    far, far_late = ([(y ^ 1, x ^ 1) for x, y in masks] for masks in (own, own_late))
    groups = (own + far, own_late, far_late)
    normed, high, low, *bias = norm_and_pool(groups, frames_in, frame_time, norm_gain)

    def send(x, pair):
        return lax.ppermute(x, "tm", [(i, i ^ pair[i % 2]) for i in range(n)])

    def project(w):
        return jnp.dot(normed, w, preferred_element_type=F32).astype(BF16)

    came = send(high, phases[0])
    query = project(w_query)
    came, normed, query = lax.optimization_barrier((came, normed, query))
    block = pl.pallas_call(
        pooled_kernel,
        out_shape=jax.ShapeDtypeStruct((2 * high.shape[0], 2 * HEADS * HD), BF16),
        in_specs=[VMEM] * 5,
        out_specs=VMEM,
        compiler_params=pltpu.CompilerParams(vmem_limit_bytes=16 << 20),
        name="pooled_keys_values",
    )(high, low, came, w_key, w_value)
    for pair in phases[1:-2]:
        block = jnp.concatenate([block, send(block, pair)], axis=0)
    brought = send(block, phases[-2])
    early = send(block, phases[-1])
    keys, values = project(w_key), project(w_value)
    brought, early, keys, values = lax.optimization_barrier((brought, early, keys, values))
    late = send(brought, phases[-1])
    block = jnp.concatenate([block, brought, early], axis=0)
    other = send(block, (1, 1))
    state = (
        jax.ShapeDtypeStruct((cols, rows), F32),
        jax.ShapeDtypeStruct((8, rows), F32),
        jax.ShapeDtypeStruct((8, rows), F32),
    )
    params = pltpu.CompilerParams(vmem_limit_bytes=32 << 20)
    acc, m, l = pl.pallas_call(
        first_kernel,
        out_shape=state,
        in_specs=[VMEM] * 6,
        out_specs=(VMEM, VMEM, VMEM),
        compiler_params=params,
        cost_estimate=pl.CostEstimate(flops=900_000_000, bytes_accessed=5_000_000, transcendentals=1_000_000),
        name="local_and_first",
    )(bias[0], query, keys, values, block, other)
    late, acc, m, l = lax.optimization_barrier((late, acc, m, l))
    other_late = send(late, (1, 1))
    acc, m, l = pl.pallas_call(
        middle_kernel,
        out_shape=state,
        in_specs=[VMEM] * 6,
        out_specs=(VMEM, VMEM, VMEM),
        input_output_aliases={3: 0, 4: 1, 5: 2},
        compiler_params=params,
        cost_estimate=pl.CostEstimate(flops=500_000_000, bytes_accessed=5_000_000, transcendentals=400_000),
        name="middle",
    )(bias[1], query, late, acc, m, l)
    return pl.pallas_call(
        last_kernel,
        out_shape=jax.ShapeDtypeStruct((rows, w_output.shape[1]), BF16),
        in_specs=[VMEM] * 7,
        out_specs=HBM,
        scratch_shapes=[
            pltpu.VMEM((rows, cols), BF16),
            pltpu.VMEM((rows, w_output.shape[1]), BF16),
            pltpu.SemaphoreType.DMA((3,)),
        ],
        compiler_params=params,
        cost_estimate=pl.CostEstimate(flops=1_700_000_000, bytes_accessed=8_000_000, transcendentals=400_000),
        name="last_and_output",
    )(bias[2], query, other_late, acc, m, l, w_output)


def solution(mesh):
    placed = (P(("grp", "tm"), None), P("grp"), P(), P(), P(), P(), P())
    return jax.shard_map(
        functools.partial(on_device, mesh.shape["tm"]),
        mesh=mesh,
        in_specs=placed,
        out_specs=P(("grp", "tm"), None),
        check_vma=False,
    )
```

```python
import functools
import math

import jax
import jax.numpy as jnp
from jax import lax
from jax.experimental import pallas as pl
from jax.experimental.pallas import tpu as pltpu
from jax.sharding import PartitionSpec as P

HEADS = 6
HD = 128
HH = 16
WW = 16
WIN = 8
POOL = 4
TOKENS = HH * WW
SLOTS = TOKENS // (POOL * POOL)
FAR = -1e30
SCALE = HD**-0.5 * math.log2(math.e)
F32 = jnp.float32
BF16 = jnp.bfloat16
VMEM = pl.BlockSpec(memory_space=pltpu.VMEM)
HBM = pl.BlockSpec(memory_space=pl.ANY)


def exchange_plan(n):
    high = [1 << b for b in range(n.bit_length() - 2, 0, -1)]
    phases = list(zip(high, high[-1:] + high[:-1]))
    held = []
    for core in range(2):
        masks = [0]
        for pair in phases[:-2]:
            masks = masks + [m ^ pair[core] for m in masks]
        before, last = phases[-2][core], phases[-1][core]
        brought = [m ^ before for m in masks]
        held.append((masks + brought + [m ^ last for m in masks], [m ^ last for m in brought]))
    return phases, held


def norm_kernel(frames_hbm, gain_hbm, normed_ref, high_ref, low_ref, x_buf, gain_buf, x_sem, g_sem):
    rows, width = x_buf.shape
    parts = x_sem.shape[0]
    step = rows // parts
    loads = [
        pltpu.make_async_copy(frames_hbm.at[pl.ds(i * step, step)], x_buf.at[pl.ds(i * step, step)], x_sem.at[i])
        for i in range(parts)
    ]
    gain_load = pltpu.make_async_copy(gain_hbm, gain_buf.at[0], g_sem)
    for copy in loads + [gain_load]:
        copy.start()
    gain_load.wait()
    gain = gain_buf[...]
    pair = 2 * WW
    for i in range(parts):
        loads[i].wait()
        for g in range(i * step // pair, (i + 1) * step // pair):
            x = x_buf[pl.ds(g * pair, pair), :].astype(F32)
            scale = lax.rsqrt(jnp.mean(x * x, axis=-1, keepdims=True) + 1e-06)
            y = x * scale * gain
            normed_ref[pl.ds(g * pair, pair), :] = y.astype(BF16)
    count = rows // TOKENS
    out_rows = count * SLOTS
    slot = lax.broadcasted_iota(jnp.int32, (out_rows, rows), 0)
    token = lax.broadcasted_iota(jnp.int32, (out_rows, rows), 1)
    home = token // (WW * POOL) * (WW // POOL) + token % WW // POOL
    pick = jnp.where(home == slot, 1.0 / (POOL * POOL), 0.0).astype(BF16)
    mean = jnp.dot(pick, normed_ref[...], preferred_element_type=F32)
    high = mean.astype(BF16)
    high_ref[...] = high
    low_ref[...] = (mean - high.astype(F32)).astype(BF16)


def mask_kernel(mask_groups, count, time_hbm, *rest):
    bias_refs, (time_ref, t_sem) = rest[:-2], rest[-2:]
    time_load = pltpu.make_async_copy(time_hbm, time_ref, t_sem)
    time_load.start()
    time_load.wait()
    for masks, bias_ref in zip(mask_groups, bias_refs):
        mask_rows(time_ref, masks, count, bias_ref)


def mask_biases(mask_groups, frame_time, count):
    return pl.pallas_call(
        functools.partial(mask_kernel, mask_groups, count),
        out_shape=tuple(jax.ShapeDtypeStruct((len(masks) * count * SLOTS, count * HD), F32) for masks in mask_groups),
        in_specs=[HBM],
        out_specs=(VMEM,) * len(mask_groups),
        scratch_shapes=[pltpu.SMEM(frame_time.shape, jnp.int32), pltpu.SemaphoreType.DMA],
        compiler_params=pltpu.CompilerParams(vmem_limit_bytes=16 << 20),
        name="mask_biases",
    )(pltpu.with_memory_space_constraint(frame_time, pltpu.HBM))


def norm_and_pool(frames, gain):
    rows, width = frames.shape
    pooled = jax.ShapeDtypeStruct((rows // TOKENS * SLOTS, width), BF16)
    return pl.pallas_call(
        norm_kernel,
        out_shape=(jax.ShapeDtypeStruct((rows, width), BF16), pooled, pooled),
        in_specs=[HBM] * 2,
        out_specs=(VMEM,) * 3,
        scratch_shapes=[
            pltpu.VMEM((rows, width), BF16),
            pltpu.VMEM((1, width), F32),
            pltpu.SemaphoreType.DMA((2,)),
            pltpu.SemaphoreType.DMA,
        ],
        compiler_params=pltpu.CompilerParams(vmem_limit_bytes=16 << 20),
        cost_estimate=pl.CostEstimate(flops=400_000_000, bytes_accessed=8_000_000, transcendentals=0),
        name="norm_and_pool",
    )(*(pltpu.with_memory_space_constraint(x, pltpu.HBM) for x in (frames, gain)))


def pooled_kernel(high_ref, low_ref, came_ref, wk_ref, wv_ref, out_ref):
    rows = high_ref.shape[0]
    x = jnp.concatenate([high_ref[...], low_ref[...], came_ref[...]], axis=0)
    cols = HEADS * HD
    for i, w_ref in enumerate((wk_ref, wv_ref)):
        z = jnp.dot(x, w_ref[...], preferred_element_type=F32)
        part = slice(i * cols, (i + 1) * cols)
        out_ref[:, part] = jnp.concatenate([z[:rows] + z[rows : 2 * rows], z[2 * rows :]], axis=0).astype(BF16)


def own_block(me, mask_pair):
    a, b = mask_pair
    return me ^ (a if a == b else jnp.where(me % 2 == 0, a, b))


def mask_rows(time_ref, masks, count, bias_ref):
    me = lax.axis_index("tm")
    own = [time_ref[me * count + f] for f in range(count)]
    for i, pair in enumerate(masks):
        source = own_block(me, pair)
        for g in range(count):
            t = time_ref[source * count + g]
            for f in range(count):
                value = jnp.where(t < own[f], 0.0, FAR).astype(F32)
                bias_ref[pl.ds((i * count + g) * SLOTS, SLOTS), head(f)] = jnp.full((SLOTS, HD), value, F32)


def mask_scores(s, bias):
    copies = TOKENS // HD
    columns = [bias[:, head(f)] for f in range(s.shape[1] // TOKENS) for _ in range(copies)]
    return s + jnp.concatenate(columns, axis=1)


def dot_nt(a, b):
    return lax.dot_general(a, b, (((1,), (1,)), ((), ())), preferred_element_type=F32)


def dot_tn(a, b):
    return lax.dot_general(a, b, (((0,), (0,)), ((), ())), preferred_element_type=F32)


def head(h, base=0):
    return slice(base + h * HD, base + (h + 1) * HD)


def first_kernel(bias_ref, q_ref, k_ref, v_ref, near_ref, other_ref, acc_ref, m_ref, l_ref):
    tokens = q_ref.shape[0]
    cols = HEADS * HD
    bias = bias_ref[...]
    band = WIN * WW
    left = lax.broadcasted_iota(jnp.int32, (WIN, band), 1) % WW < WIN
    bands = [slice(t, t + band) for t in range(0, tokens, band)]

    def scores(h):
        q = q_ref[:, head(h)]
        far_k = jnp.concatenate([near_ref[:, head(h)], other_ref[:, head(h)]], axis=0)
        far_s = mask_scores(dot_nt(far_k, q), bias)
        parts = []
        for two in bands:
            s = dot_nt(k_ref[two, head(h)], q_ref[two, head(h)])
            lines = [jnp.where(left, s[r : r + WIN], s[r + WIN : r + WW]) for r in range(0, band, WW)]
            parts.append(jnp.concatenate(lines, axis=0))
        return jnp.concatenate(parts, axis=1), far_s

    def weigh(h, local_s, far_s):
        top = jnp.maximum(jnp.max(local_s, axis=0, keepdims=True), jnp.max(far_s, axis=0, keepdims=True))
        local_w = jnp.exp2((local_s - top) * SCALE)
        far_w = jnp.exp2((far_s - top) * SCALE)
        m_ref[h : h + 1, :] = top
        l_ref[h : h + 1, :] = jnp.sum(local_w, axis=0, keepdims=True) + jnp.sum(far_w, axis=0, keepdims=True)
        return local_w, far_w.astype(BF16)

    def mix(h, local_w, far_w):
        far_v = jnp.concatenate([near_ref[:, head(h, cols)], other_ref[:, head(h, cols)]], axis=0)
        acc = dot_tn(far_v, far_w)
        for two in bands:
            lines = []
            for r in range(0, WIN * WIN, WIN):
                p = local_w[r : r + WIN, two]
                lines += [jnp.where(left, p, 0.0), jnp.where(left, 0.0, p)]
            p = jnp.concatenate(lines, axis=0).astype(BF16)
            acc_ref[head(h), two] = acc[:, two] + dot_tn(v_ref[two, head(h)], p)

    pipelined(scores, weigh, mix)


def pipelined(scores, weigh, mix):
    ahead = 2
    ready = {h: scores(h) for h in range(ahead)}
    weights = {}
    for h in range(HEADS):
        if h + ahead < HEADS:
            ready[h + ahead] = scores(h + ahead)
        weights[h] = weigh(h, *ready.pop(h))
        if h > 0:
            mix(h - 1, *weights.pop(h - 1))
    mix(HEADS - 1, *weights.pop(HEADS - 1))


def far_stages(bias_ref, q_ref, far_ref, m_in, l_in, acc_in, keep_state, keep_acc):
    cols = HEADS * HD
    bias = bias_ref[...]

    def scores(h):
        return (mask_scores(dot_nt(far_ref[:, head(h)], q_ref[:, head(h)]), bias),)

    def weigh(h, s):
        m, l = m_in[h : h + 1, :], l_in[h : h + 1, :]
        top = jnp.maximum(m, jnp.max(s, axis=0, keepdims=True))
        w = jnp.exp2((s - top) * SCALE)
        keep = jnp.exp2((m - top) * SCALE)
        total = l * keep + jnp.sum(w, axis=0, keepdims=True)
        return w.astype(BF16), keep, keep_state(h, top, total)

    def mix(h, w, keep, state):
        keep_acc(h, acc_in[head(h), :] * keep + dot_tn(far_ref[:, head(h, cols)], w), state)

    pipelined(scores, weigh, mix)


def middle_kernel(bias_ref, q_ref, far_ref, acc_in, m_in, l_in, acc_ref, m_ref, l_ref):
    def keep_state(h, top, total):
        m_ref[h : h + 1, :] = top
        l_ref[h : h + 1, :] = total

    def keep_acc(h, acc, _):
        acc_ref[head(h), :] = acc

    far_stages(bias_ref, q_ref, far_ref, m_in, l_in, acc_in, keep_state, keep_acc)


def last_kernel(
    bias_ref, q_ref, far_ref, acc_in, m_in, l_in, wo_ref, out_hbm, rows_buf, out_buf, out_sem
):
    def keep_acc(h, acc, inverse):
        rows_buf[:, head(h)] = jnp.transpose((acc * inverse).astype(BF16))

    far_stages(
        bias_ref, q_ref, far_ref, m_in, l_in, acc_in, lambda h, top, total: 1.0 / total, keep_acc
    )
    tall, wide = out_sem.shape
    height, width = out_buf.shape[0] // tall, out_buf.shape[1] // wide
    copies = []
    for r in range(tall):
        for c in range(wide):
            rows, part = pl.ds(r * height, height), pl.ds(c * width, width)
            out = jnp.dot(rows_buf[rows, :], wo_ref[:, part], preferred_element_type=F32)
            out_buf[rows, part] = out.astype(BF16)
            copies.append(
                pltpu.make_async_copy(out_buf.at[rows, part], out_hbm.at[rows, part], out_sem.at[r, c])
            )
            copies[-1].start()
    for copy in copies:
        copy.wait()


def on_device(n, frames_in, frame_time, norm_gain, w_query, w_key, w_value, w_output):
    rows = frames_in.shape[0]
    cols = HEADS * HD
    phases, held = exchange_plan(n)
    own, own_late = (list(zip(x, y)) for x, y in zip(*held))
    far, far_late = ([(y ^ 1, x ^ 1) for x, y in masks] for masks in (own, own_late))
    groups = (own + far, own_late, far_late)
    normed, high, low = norm_and_pool(frames_in, norm_gain)

    def send(x, pair):
        return lax.ppermute(x, "tm", [(i, i ^ pair[i % 2]) for i in range(n)])

    def project(w):
        return jnp.dot(normed, w, preferred_element_type=F32).astype(BF16)

    came = send(high, phases[0])
    query = project(w_query)
    came, normed, query, frame_time = lax.optimization_barrier((came, normed, query, frame_time))
    block = pl.pallas_call(
        pooled_kernel,
        out_shape=jax.ShapeDtypeStruct((2 * high.shape[0], 2 * HEADS * HD), BF16),
        in_specs=[VMEM] * 5,
        out_specs=VMEM,
        compiler_params=pltpu.CompilerParams(vmem_limit_bytes=16 << 20),
        name="pooled_keys_values",
    )(high, low, came, w_key, w_value)
    for pair in phases[1:-2]:
        block = jnp.concatenate([block, send(block, pair)], axis=0)
    bias = mask_biases(groups, frame_time, rows // TOKENS)
    brought = send(block, phases[-2])
    early = send(block, phases[-1])
    keys, values = project(w_key), project(w_value)
    brought, early, keys, values = lax.optimization_barrier((brought, early, keys, values))
    late = send(brought, phases[-1])
    block = jnp.concatenate([block, brought, early], axis=0)
    other = send(block, (1, 1))
    state = (
        jax.ShapeDtypeStruct((cols, rows), F32),
        jax.ShapeDtypeStruct((8, rows), F32),
        jax.ShapeDtypeStruct((8, rows), F32),
    )
    params = pltpu.CompilerParams(vmem_limit_bytes=32 << 20)
    acc, m, l = pl.pallas_call(
        first_kernel,
        out_shape=state,
        in_specs=[VMEM] * 6,
        out_specs=(VMEM, VMEM, VMEM),
        compiler_params=params,
        cost_estimate=pl.CostEstimate(flops=900_000_000, bytes_accessed=5_000_000, transcendentals=1_000_000),
        name="local_and_first",
    )(bias[0], query, keys, values, block, other)
    late, acc, m, l = lax.optimization_barrier((late, acc, m, l))
    other_late = send(late, (1, 1))
    acc, m, l = pl.pallas_call(
        middle_kernel,
        out_shape=state,
        in_specs=[VMEM] * 6,
        out_specs=(VMEM, VMEM, VMEM),
        input_output_aliases={3: 0, 4: 1, 5: 2},
        compiler_params=params,
        cost_estimate=pl.CostEstimate(flops=500_000_000, bytes_accessed=5_000_000, transcendentals=400_000),
        name="middle",
    )(bias[1], query, late, acc, m, l)
    return pl.pallas_call(
        last_kernel,
        out_shape=jax.ShapeDtypeStruct((rows, w_output.shape[1]), BF16),
        in_specs=[VMEM] * 7,
        out_specs=HBM,
        scratch_shapes=[
            pltpu.VMEM((rows, cols), BF16),
            pltpu.VMEM((rows, w_output.shape[1]), BF16),
            pltpu.SemaphoreType.DMA((2, 3)),
        ],
        compiler_params=params,
        cost_estimate=pl.CostEstimate(flops=1_700_000_000, bytes_accessed=8_000_000, transcendentals=400_000),
        name="last_and_output",
    )(bias[2], query, other_late, acc, m, l, w_output)


def solution(mesh):
    placed = (P(("grp", "tm"), None), P("grp"), P(), P(), P(), P(), P())
    return jax.shard_map(
        functools.partial(on_device, mesh.shape["tm"]),
        mesh=mesh,
        in_specs=placed,
        out_specs=P(("grp", "tm"), None),
        check_vma=False,
    )
```
